512 devices in a mesh: dp: 16 (over x, z_hi, core), expert: 32 (over z_lo, y).
Axes of the slice: x: 4, y: 8, z: 8 (z_hi: 2, z_lo: 4; z = z_hi * 4 + z_lo), core: 2. Of those that a mesh axis runs over, the one named last changes fastest.
Arguments:
- tokens_in: bfloat16 [65536, 4096], P(('dp', 'expert')), may hold values from -6 to 6
- out_grad: bfloat16 [65536, 4096], P(('dp', 'expert')), may hold values from -6 to 6
- routes: int32 [65536, 2], P(('dp', 'expert')), may hold values from 0 to 31, as said below
- router_probs: float32 [65536, 2], P(('dp', 'expert')), may hold values from 0.1 to 1
- gate_up: bfloat16 [2, 4096, 4096], P(None, 'expert', 'dp'), may hold values from -0.09375 to 0.09375
- down_proj: bfloat16 [4096, 4096], P('expert', 'dp'), may hold values from -0.09375 to 0.09375
Outputs:
- in_grad: bfloat16 [65536, 4096], P(('dp', 'expert'))
- grad_gate_up: float32 [2, 4096, 4096], P(None, 'expert', 'dp')
- grad_down: float32 [4096, 4096], P('expert', 'dp')
The draws below stay inside these ranges and needn't reach their ends.
Inputs may be any that keep to these rules, and one draw needn't show every extreme that they name: `routes`: each row names two different experts. Expert 0 is the expert in the window: each token names it at most once, the tokens of one device (an aligned block of 128 rows) name it at most 8 times, and on every device of one index of dp (which index varies by draw) exactly 8 times; devices of the other indices of dp may hold fewer.
All inputs are finite; a program needn't handle non-finite values.
Results may differ from the reference program's by a relative error of at most 0.015.
Values may be sent and summed in bfloat16 or wider, within the bound.
A program may use at most 64 MiB of HBM per device.

```python
import jax
import jax.numpy as jnp
from jax import lax

D = 4096
FW = 4096
EXPERTS = 32
TOK_DEV = 128
CAP = 8
ROWS = 256
UNITS = 128
TOKENS = 65536
N_DP = 16
N_EXPERT = 32


def draw_routes(key, part):
    key = jax.random.fold_in(key, 11)
    keys = jax.random.split(key, 6)
    blocks = TOKENS // TOK_DEV
    first = jax.random.randint(keys[0], (TOKENS,), 1, EXPERTS)
    second = 1 + (first - 1 + jax.random.randint(keys[1], (TOKENS,), 1, EXPERTS - 1)) % (EXPERTS - 1)
    counts = jax.random.randint(keys[2], (blocks,), 1, CAP + 1)
    busiest = jax.random.randint(keys[3], (), 0, N_DP)
    group = jnp.arange(blocks) // (blocks // N_DP)
    counts = jnp.where(group == busiest, CAP, counts)
    ranks = jax.vmap(lambda k: jax.random.permutation(k, TOK_DEV))(jax.random.split(keys[4], blocks))
    picked = (ranks < counts[:, None]).reshape(-1)
    column = jax.random.randint(keys[5], (TOKENS,), 0, 2)
    left = jnp.where(picked & (column == 0), 0, first)
    right = jnp.where(picked & (column == 1), 0, second)
    return jnp.stack([left, right], axis=1).astype(jnp.int32)


def shard_levels(key, extent, cuts, low, high):
    factor_of, own = 1.0, jax.random.fold_in(key, 6)
    for axis_at, blocks in cuts:
        draws = jnp.exp(jax.random.uniform(jax.random.fold_in(own, axis_at), (blocks,), jnp.float32, low / len(cuts), high / len(cuts)))
        factor_of = factor_of * jnp.repeat(draws, extent[axis_at] // blocks).reshape([-1 if axis == axis_at else 1 for axis in range(len(extent))])
    return factor_of


def noise(own_key, shape, width, bound, cuts=(), held_as=jnp.bfloat16):
    level = shard_levels(own_key, shape, cuts, -0.22, 0.18) if cuts else 1.0
    values = jax.random.normal(own_key, shape, jnp.float32) * width * level
    return jnp.minimum(jnp.maximum(values, -bound), bound).astype(held_as)


def setup_inputs(seed: int = 0) -> dict:
    key_of = jax.random.split(jax.random.key(seed), 7)
    tokens_in = noise(key_of[0], (TOKENS, D), 1.0, 6.0, ((0, 512),))
    out_grad = noise(key_of[1], (TOKENS, D), 1.0, 6.0, ((0, 512),))
    routes = draw_routes(jax.random.fold_in(key_of[6], 71), 0)
    router_probs = jnp.clip(0.1 + 0.9 * jax.random.uniform(key_of[3], (TOKENS, 2), jnp.float32) ** shard_levels(key_of[3], (TOKENS, 2), ((0, 512),), -0.2, 0.2), 0.1, 1.0)
    gate_up = noise(key_of[4], (2, FW, D), D ** -0.5, 0.09375, ((1, 32), (2, 16)))
    down_proj = noise(key_of[5], (FW, D), FW ** -0.5, 0.09375, ((0, 32), (1, 16)))
    return {"tokens_in": tokens_in, "out_grad": out_grad, "routes": routes, "router_probs": router_probs, "gate_up": gate_up, "down_proj": down_proj}


def reference(tokens_in, out_grad, routes, router_probs, gate_up, down_proj):
    blocks = N_DP * N_EXPERT
    chosen = routes == 0
    weight = jnp.sum(jnp.where(chosen, router_probs, jnp.float32(0.0)), axis=1)
    member = jnp.any(chosen, axis=1).reshape(blocks, TOK_DEV)
    position = jnp.cumsum(member.astype(jnp.int32), axis=1) - 1
    slot_ids = jnp.arange(CAP, dtype=jnp.int32)
    placed = (position[:, None, :] == slot_ids[None, :, None]) & member[:, None, :]
    local_ids = jnp.arange(TOK_DEV, dtype=jnp.int32)
    local_index = jnp.sum(jnp.where(placed, local_ids[None, None, :], 0), axis=2).astype(jnp.int32)
    filled = jnp.any(placed, axis=2).reshape(-1)
    block_base = (jnp.arange(blocks, dtype=jnp.int32) * TOK_DEV)[:, None]
    token_index = (local_index + block_base).reshape(-1).astype(jnp.int32)
    read_index = jnp.where(filled, token_index, 0).astype(jnp.int32)
    write_index = jnp.where(filled, token_index, TOKENS).astype(jnp.int32)
    picked_weight = weight[read_index]
    scaled_rows = (picked_weight[:, None] * out_grad[read_index].astype(jnp.float32)).astype(jnp.bfloat16)
    zero_row = jnp.zeros((), jnp.bfloat16)
    x_rows = jnp.where(filled[:, None], tokens_in[read_index], zero_row).reshape(N_DP, ROWS, D)
    e_rows = jnp.where(filled[:, None], scaled_rows, zero_row).reshape(N_DP, ROWS, D)
    gate_w = gate_up[0]
    up_w = gate_up[1]

    def group_step(carry, items):
        rows_x, rows_e = items
        gate_pre = jnp.dot(rows_x, gate_w.T, preferred_element_type=jnp.float32)
        up_pre = jnp.dot(rows_x, up_w.T, preferred_element_type=jnp.float32)
        hidden_grad = jnp.dot(rows_e, down_proj.T, preferred_element_type=jnp.float32)
        sigmoid_gate = jax.nn.sigmoid(gate_pre)
        activated = gate_pre * sigmoid_gate
        hidden = (activated * up_pre).astype(jnp.bfloat16)
        up_grad = (hidden_grad * activated).astype(jnp.bfloat16)
        gate_grad = (hidden_grad * up_pre * sigmoid_gate * (1.0 + gate_pre * (1.0 - sigmoid_gate))).astype(jnp.bfloat16)

        def unit_step(total, index):
            start = (index * UNITS).astype(jnp.int32)
            piece_gate = lax.dynamic_slice_in_dim(gate_grad, start, UNITS, 1)
            piece_up = lax.dynamic_slice_in_dim(up_grad, start, UNITS, 1)
            rows_gate = lax.dynamic_slice_in_dim(gate_w, start, UNITS, 0)
            rows_up = lax.dynamic_slice_in_dim(up_w, start, UNITS, 0)
            part = jnp.dot(piece_gate, rows_gate, preferred_element_type=jnp.float32)
            part = part + jnp.dot(piece_up, rows_up, preferred_element_type=jnp.float32)
            part = part.astype(jnp.bfloat16)
            return total + part.astype(jnp.float32), None

        row_grad, _ = lax.scan(unit_step, jnp.zeros((ROWS, D), jnp.float32), jnp.arange(N_EXPERT, dtype=jnp.int32))
        pair_part = jnp.stack([
            jnp.dot(gate_grad.T, rows_x, preferred_element_type=jnp.float32),
            jnp.dot(up_grad.T, rows_x, preferred_element_type=jnp.float32)]).astype(jnp.bfloat16)
        down_part = jnp.dot(hidden.T, rows_e, preferred_element_type=jnp.float32).astype(jnp.bfloat16)
        pair_part, down_part = lax.optimization_barrier((pair_part, down_part))
        carry = (carry[0] + pair_part.astype(jnp.float32), carry[1] + down_part.astype(jnp.float32))
        return carry, row_grad.astype(jnp.bfloat16)

    start_carry = (jnp.zeros((2, FW, D), jnp.float32), jnp.zeros((FW, D), jnp.float32))
    grads, row_grads = lax.scan(group_step, start_carry, (x_rows, e_rows))
    row_grads = row_grads.reshape(N_DP * ROWS, D)
    in_grad = jnp.zeros((TOKENS, D), jnp.bfloat16).at[write_index].set(row_grads, mode="drop")
    return in_grad, grads[0], grads[1]
```

```python
import jax
import jax.numpy as jnp
from jax import lax
from jax.experimental import pallas as pl
from jax.experimental.pallas import tpu as pltpu
from jax.sharding import PartitionSpec as P

MESH = pl.DeviceIdType.MESH
F32, BF16 = jnp.float32, jnp.bfloat16
NX, NY, NZ = 4, 8, 4
D = 4096
CAP = 8
COLS = 256
UNITS = 128
HALF = 3 * UNITS // 2


class Sems:
    def __init__(self, send, recv):
        self.send, self.recv, self.used = send, recv, 0

    def take(self, n=1):
        at = self.used
        self.used += n
        return at


def kernel(
    tok_hbm, og_hbm, routes, probs, gu_hbm, dn_hbm,
    out_tok, out_gu, out_dn,
    tok, og, G, W, A_t, dH, R, yrecv, zrecv, T, crecv, xrecv, zhrecv, zhsend,
    load_sem, send_sem, recv_sem,
):
    dp, ex = lax.axis_index("dp"), lax.axis_index("expert")
    x, zh, c = dp // 4, (dp // 2) % 2, dp % 2
    zl, y = ex // NY, ex % NY

    def at(x=x, zh=zh, c=c, zl=zl, y=y):
        return ((x * 2 + zh) * 2 + c, zl * NY + y)

    right, left = at(x=(x + 1) % NX), at(x=(x + NX - 1) % NX)
    north, south = at(y=(y + 1) % NY), at(y=(y + NY - 1) % NY)
    other_core, other_run = at(c=1 - c), at(zh=1 - zh)
    in_run = [at(zl=(zl + j) % NZ) for j in range(1, NZ)]

    barrier = pltpu.get_barrier_semaphore()
    peers = [right, left, north, south, other_core, other_run] + in_run
    for peer in peers:
        pl.semaphore_signal(barrier, inc=1, device_id=peer, device_id_type=MESH)

    def cols(i):
        return pl.ds(pl.multiple_of(i * COLS, COLS), COLS)

    mine = cols(dp)
    loads = [
        pltpu.make_async_copy(tok_hbm, tok, load_sem.at[0]),
        pltpu.make_async_copy(og_hbm, og, load_sem.at[1]),
        pltpu.make_async_copy(gu_hbm.at[0], W.at[pl.ds(0, UNITS), mine], load_sem.at[2]),
        pltpu.make_async_copy(gu_hbm.at[1], W.at[pl.ds(UNITS, UNITS), mine], load_sem.at[3]),
        pltpu.make_async_copy(dn_hbm, W.at[pl.ds(2 * UNITS, UNITS), mine], load_sem.at[4]),
    ]
    for load in loads:
        load.start()

    n_tok = tok.shape[0]
    chosen = routes[...] == 0
    weight = jnp.sum(jnp.where(chosen, probs[...], 0.0), axis=1, keepdims=True)
    member = jnp.sum(jnp.where(chosen, 1.0, 0.0), axis=1, keepdims=True)
    member_l = jnp.broadcast_to(member, (n_tok, n_tok)).T[: 2 * CAP]
    weight_l = jnp.broadcast_to(weight, (n_tok, n_tok)).T[: 2 * CAP]
    before = lax.broadcasted_iota(jnp.int32, (n_tok, n_tok), 0)
    upto = lax.broadcasted_iota(jnp.int32, (n_tok, n_tok), 1)
    prefix = jnp.where(before <= upto, 1.0, 0.0).astype(BF16)
    position = jnp.dot(member_l.astype(BF16), prefix, preferred_element_type=F32)
    slot = (lax.broadcasted_iota(jnp.int32, (2 * CAP, n_tok), 0) % CAP).astype(F32)
    picker = jnp.where((position - 1.0 == slot) & (member_l > 0.5), 1.0, 0.0)
    slot_weight = jnp.sum(picker * weight_l, axis=1, keepdims=True)
    picker_b = picker.astype(BF16)
    own_block = y * NZ + zl
    for load in loads:
        load.wait()
    x_rows = jnp.dot(picker_b, tok[...], preferred_element_type=F32)
    g_rows = jnp.dot(picker_b, og[...], preferred_element_type=F32)
    e_rows = slot_weight * g_rows
    G[own_block] = jnp.concatenate([x_rows[:CAP], e_rows[CAP:]], axis=0).astype(BF16)

    pl.semaphore_wait(barrier, len(peers))

    sems = Sems(send_sem, recv_sem)
    sent = []

    def copy(src, dst, device, k):
        return pltpu.make_async_remote_copy(
            src_ref=src,
            dst_ref=dst,
            send_sem=send_sem.at[k],
            recv_sem=recv_sem.at[k],
            device_id=device,
            device_id_type=MESH,
        )

    def go(src, dst, device, k=None):
        one = copy(src, dst, device, sems.take() if k is None else k)
        one.start()
        sent.append(one)
        return one

    upper = zl // 2
    m = zl * (1 - upper) + (3 - zl) * upper
    order = [b * (1 - upper) + (3 - b) * upper for b in (m, 1 - m, 2, 3)]

    z_up, z_down = sems.take(NZ), sems.take(NZ)
    z_sent = []

    def z_copy(zs, up):
        ref = G.at[y * NZ + zs]
        return pltpu.make_async_remote_copy(
            src_ref=ref,
            dst_ref=ref,
            send_sem=send_sem.at[(z_up if up else z_down) + zs],
            recv_sem=recv_sem.at[z_up + zs],
            device_id=at(zl=(zl + (1 if up else NZ - 1)) % NZ),
            device_id_type=MESH,
        )

    def z_forward(zs):
        @pl.when((zs <= zl) & (zl < NZ - 1))
        def _():
            z_copy(zs, True).start()

        @pl.when((zs >= zl) & (zl > 0))
        def _():
            z_copy(zs, False).start()

        z_sent.append(zs)

    def hops(k, plus):
        return 4 if (k in (0, 3)) == plus else 3

    y_live = {}

    def y_send(k, h, plus):
        src_y = (y + (NY - h + 1 if plus else h - 1)) % NY
        ref = G.at[src_y * NZ + order[k]]
        y_live[k, h, plus] = go(ref, ref, north if plus else south)

    def y_step(k, h):
        for plus in (True, False):
            if 1 <= h - 1 <= hops(k, plus):
                y_live[k, h - 1, plus].wait_recv()
            if h <= hops(k, plus):
                y_send(k, h, plus)

    def block_of(xx, zz, cc):
        return (xx * 2 + zz) * 2 + cc

    def w_ref(xx, zz, rows=pl.ds(0, 3 * UNITS), cc=c):
        return W.at[rows, cols(block_of(xx, zz, cc))]

    lo, hi = pl.ds(0, HALF), pl.ds(HALF, HALF)
    x1, x2, x3 = (x + 1) % NX, (x + 2) % NX, (x + 3) % NX
    to_core = []

    def w_core(xx, zz):
        to_core.append(go(w_ref(xx, zz), w_ref(xx, zz), other_core))

    def w_hop1(zz):
        ref = w_ref(x, zz)
        return go(ref, ref, right), go(ref, ref, left)

    def w_hop2(zz, first):
        first[0].wait_recv()
        a = go(w_ref(x3, zz, lo), w_ref(x3, zz, lo), right)
        first[1].wait_recv()
        b = go(w_ref(x1, zz, hi), w_ref(x1, zz, hi), left)
        w_core(x3, zz)
        w_core(x1, zz)
        return a, b

    def w_last(zz, second):
        second[0].wait_recv()
        second[1].wait_recv()
        w_core(x2, zz)

    z_forward(order[0])
    y_step(0, 1)
    w_run = go(w_ref(x, zh), w_ref(x, zh), other_run)
    first_a = w_hop1(zh)
    w_core(x, zh)
    for t in range(1, 8):
        for k in range(4):
            h = t - k + 1
            if h == 1:
                z_copy(order[k], True).wait_recv()
                z_forward(order[k])
            if 1 <= h <= 5:
                y_step(k, h)
        if t == 1:
            second_a = w_hop2(zh, first_a)
        if t == 3:
            w_run.wait_recv()
            first_b = w_hop1(1 - zh)
            w_core(x, 1 - zh)
            w_last(zh, second_a)
        if t == 5:
            second_b = w_hop2(1 - zh, first_b)
        if t == 7:
            w_last(1 - zh, second_b)
    for one in to_core:
        one.wait_recv()

    for half in range(2):
        g = G[pl.ds(half * 16, 16)].reshape(256, D)
        pre = lax.dot_general(g, W[...], (((1,), (1,)), ((), ())), preferred_element_type=F32)
        pre = pre.reshape(16, 2 * CAP, 3 * UNITS)
        gate_pre = pre[:, :CAP, :UNITS]
        up_pre = pre[:, :CAP, UNITS : 2 * UNITS]
        hidden_grad = pre[:, CAP:, 2 * UNITS :]
        sig = 1.0 / (1.0 + jnp.exp(-gate_pre))
        activated = gate_pre * sig
        hidden = activated * up_pre
        up_grad = hidden_grad * activated
        gate_grad = hidden_grad * up_pre * sig * (1.0 + gate_pre * (1.0 - sig))
        zero = jnp.zeros_like(hidden)
        a = jnp.concatenate(
            [
                jnp.concatenate([gate_grad, up_grad, zero], axis=2),
                jnp.concatenate([zero, zero, hidden], axis=2),
            ],
            axis=1,
        ).reshape(256, 3 * UNITS)
        A_t[:, pl.ds(half * 256, 256)] = a.T.astype(BF16)
        grads = jnp.concatenate([gate_grad, up_grad], axis=2).reshape(128, 2 * UNITS)
        dH[pl.ds(half * 128, 128)] = grads.astype(BF16)

    def weight_grad(i):
        g = G[:, :, cols(i)].reshape(512, COLS)
        T[i] = jnp.dot(A_t[...], g, preferred_element_type=F32).astype(BF16)

    x_order = [x2, x1, x3, x]
    core_copies = []
    for n, xx in enumerate(x_order):
        for zz in range(2):
            i = block_of(xx, zz, 1 - c)
            weight_grad(i)
            core_copies.append(go(T.at[i], crecv.at[2 * n + zz], other_core))

    WIDE = 512
    for j in range(D // 2 // WIDE):
        parts = []
        for base in (0, D // 2):
            w = W[pl.ds(0, 2 * UNITS), pl.ds(base + j * WIDE, WIDE)]
            part = jnp.dot(dH[...], w, preferred_element_type=F32)
            parts.append(part.reshape(NY * NZ, CAP, WIDE))
        both = jnp.concatenate(parts, axis=1).astype(BF16)
        R[:, :, :, pl.ds(j * WIDE, WIDE)] = both.reshape(NY, NZ, 2 * CAP, WIDE)

    PART = D // 4

    def r_part(yy, p):
        return R.at[yy, :, :, pl.ds(p * PART, PART)]

    def r_hops(p, plus):
        return 4 if (p == 0) == plus else 3

    r_slot = {}
    for plus in (True, False):
        for p in range(2):
            for s in range(1, r_hops(p, plus) + 1):
                r_slot[p, s, plus] = len(r_slot)
    r_live = {}

    def r_dest(p, s, plus):
        d = r_hops(p, plus) - s + 1
        return (y + (d if plus else NY - d)) % NY

    def r_send(p, s, plus):
        r_live[p, s, plus] = go(
            r_part(r_dest(p, s, plus), p),
            yrecv.at[r_slot[p, s, plus]],
            north if plus else south,
        )

    def r_step(p, s, plus):
        r_live[p, s, plus].wait_recv()
        dest = r_dest(p, s + 1, plus)
        ref = r_part(dest, p)
        total = ref[...].astype(F32) + yrecv[r_slot[p, s, plus]].astype(F32)
        ref[...] = total.astype(BF16)
        r_send(p, s + 1, plus)

    for p, plus in ((0, True), (1, False), (1, True), (0, False)):
        r_send(p, 1, plus)

    for n, xx in enumerate(x_order):
        for zz in range(2):
            weight_grad(block_of(xx, zz, c))

    def core_sum(n, zz):
        core_copies[2 * n + zz].wait_recv()
        i = block_of(x_order[n], zz, c)
        T[i] = (T[i].astype(F32) + crecv[2 * n + zz].astype(F32)).astype(BF16)

    def t_ref(xx, zz):
        return T.at[block_of(xx, zz, c)]

    core_sum(0, 0)
    xp1 = go(t_ref(x2, 0), xrecv.at[0], right)
    core_sum(0, 1)
    xm1 = go(t_ref(x2, 1), xrecv.at[1], left)
    core_sum(1, 1)
    xp2 = go(t_ref(x1, 1), xrecv.at[2], right)
    core_sum(2, 0)
    xm2 = go(t_ref(x3, 0), xrecv.at[3], left)
    core_sum(1, 0)
    core_sum(2, 1)
    core_sum(3, 0)
    core_sum(3, 1)

    for p, plus in ((0, True), (1, False), (1, True), (0, False)):
        r_step(p, 1, plus)

    xp1.wait_recv()
    i = block_of(x1, 0, c)
    T[i] = (T[i].astype(F32) + xrecv[0].astype(F32)).astype(BF16)
    xp3 = go(t_ref(x1, 0), xrecv.at[4], right)
    xm1.wait_recv()
    i = block_of(x3, 1, c)
    T[i] = (T[i].astype(F32) + xrecv[1].astype(F32)).astype(BF16)
    xm3 = go(t_ref(x3, 1), xrecv.at[5], left)

    for p, plus in ((0, True), (1, False), (1, True), (0, False)):
        r_step(p, 2, plus)

    for one in (xp2, xm2, xp3, xm3):
        one.wait_recv()
    i = block_of(x, 1 - zh, c)
    from_left = xrecv[4 - 2 * (1 - zh)].astype(F32)
    from_right = xrecv[3 + 2 * (1 - zh)].astype(F32)
    zhsend[...] = (T[i].astype(F32) + from_left + from_right).astype(BF16)
    zh_copy = go(zhsend, zhrecv, other_run)

    for p, plus in ((0, True), (1, False)):
        r_step(p, 3, plus)

    z_live = []
    for p in range(2):
        for plus in (True, False):
            r_live[p, r_hops(p, plus), plus].wait_recv()
        ref = r_part(y, p)
        total = ref[...].astype(F32)
        for plus in (True, False):
            total = total + yrecv[r_slot[p, r_hops(p, plus), plus]].astype(F32)
        ref[...] = total.astype(BF16)
        base = sems.take(NZ)
        for j in range(1, NZ):
            zs = (zl + j) % NZ
            one = pltpu.make_async_remote_copy(
                src_ref=R.at[y, zs, :, pl.ds(p * PART, PART)],
                dst_ref=zrecv.at[p, zl],
                send_sem=send_sem.at[base + zs],
                recv_sem=recv_sem.at[base + zl],
                device_id=at(zl=zs),
                device_id_type=MESH,
            )
            one.start()
            sent.append(one)
        z_live.append(base)

    i = block_of(x, zh, c)
    total = T[i].astype(F32)
    total = total + xrecv[4 - 2 * zh].astype(F32) + xrecv[3 + 2 * zh].astype(F32)
    zh_copy.wait_recv()
    total = total + zhrecv[...].astype(F32)
    out_gu[0] = total[:UNITS]
    out_gu[1] = total[UNITS : 2 * UNITS]
    out_dn[...] = total[2 * UNITS :]

    placed = jnp.concatenate([picker, jnp.zeros((n_tok - 2 * CAP, n_tok), F32)], axis=0).T
    lane = lax.broadcasted_iota(jnp.int32, (n_tok, 2 * CAP), 1)
    placed = placed[:, : 2 * CAP]
    low = jnp.where(lane < CAP, placed, 0.0).astype(BF16)
    high = jnp.where(lane >= CAP, placed, 0.0).astype(BF16)
    for p in range(2):
        total = R[y, zl, :, pl.ds(p * PART, PART)].astype(F32)
        for j in range(1, NZ):
            zs = (zl + j) % NZ
            pltpu.make_async_remote_copy(
                src_ref=zrecv.at[p, zs],
                dst_ref=zrecv.at[p, zs],
                send_sem=send_sem.at[z_live[p] + zs],
                recv_sem=recv_sem.at[z_live[p] + zs],
                device_id=at(zl=zs),
                device_id_type=MESH,
            ).wait_recv()
            total = total + zrecv[p, zs].astype(F32)
        rows = total.astype(BF16)
        for part, base in ((low, 0), (high, D // 2)):
            grad = jnp.dot(part, rows, preferred_element_type=F32)
            out_tok[:, pl.ds(base + p * PART, PART)] = grad.astype(BF16)

    for one in sent:
        one.wait_send()
    for zs in z_sent:

        @pl.when((zs <= zl) & (zl < NZ - 1))
        def _():
            z_copy(zs, True).wait_send()

        @pl.when((zs >= zl) & (zl > 0))
        def _():
            z_copy(zs, False).wait_send()


def on_device(tokens_in, out_grad, routes, router_probs, gate_up, down_proj):
    vmem = pl.BlockSpec(memory_space=pltpu.VMEM)
    anywhere = pl.BlockSpec(memory_space=pl.ANY)
    n_tok = tokens_in.shape[0]
    blocks = NY * NZ
    n_sems = 160
    return pl.pallas_call(
        kernel,
        out_shape=(
            jax.ShapeDtypeStruct(tokens_in.shape, BF16),
            jax.ShapeDtypeStruct(gate_up.shape, F32),
            jax.ShapeDtypeStruct(down_proj.shape, F32),
        ),
        in_specs=[anywhere, anywhere, vmem, vmem, anywhere, anywhere],
        out_specs=(vmem, vmem, vmem),
        scratch_shapes=[
            pltpu.VMEM((n_tok, D), BF16),
            pltpu.VMEM((n_tok, D), BF16),
            pltpu.VMEM((blocks, 2 * CAP, D), BF16),
            pltpu.VMEM((3 * UNITS, D), BF16),
            pltpu.VMEM((3 * UNITS, 2 * CAP * blocks), BF16),
            pltpu.VMEM((CAP * blocks, 2 * UNITS), BF16),
            pltpu.VMEM((NY, NZ, 2 * CAP, D // 2), BF16),
            pltpu.VMEM((14, NZ, 2 * CAP, D // 4), BF16),
            pltpu.VMEM((2, NZ, 2 * CAP, D // 4), BF16),
            pltpu.VMEM((16, 3 * UNITS, COLS), BF16),
            pltpu.VMEM((8, 3 * UNITS, COLS), BF16),
            pltpu.VMEM((6, 3 * UNITS, COLS), BF16),
            pltpu.VMEM((3 * UNITS, COLS), BF16),
            pltpu.VMEM((3 * UNITS, COLS), BF16),
            pltpu.SemaphoreType.DMA((5,)),
            pltpu.SemaphoreType.DMA((n_sems,)),
            pltpu.SemaphoreType.DMA((n_sems,)),
        ],
        compiler_params=pltpu.CompilerParams(
            collective_id=0, has_side_effects=True, vmem_limit_bytes=48 * 2**20
        ),
        cost_estimate=pl.CostEstimate(
            flops=6 * 10**9, bytes_accessed=4 * 2**20, transcendentals=2**15
        ),
        name="expert_backward",
    )(tokens_in, out_grad, routes, router_probs, gate_up, down_proj)


def solution(mesh):
    in_specs = (
        P(("dp", "expert"), None),
        P(("dp", "expert"), None),
        P(("dp", "expert"), None),
        P(("dp", "expert"), None),
        P(None, "expert", "dp"),
        P("expert", "dp"),
    )
    out_specs = (P(("dp", "expert"), None), P(None, "expert", "dp"), P("expert", "dp"))
    return jax.shard_map(
        on_device, mesh=mesh, in_specs=in_specs, out_specs=out_specs, check_vma=False
    )
```

```python
import jax
import jax.numpy as jnp
from jax import lax
from jax.experimental import pallas as pl
from jax.experimental.pallas import tpu as pltpu
from jax.sharding import PartitionSpec as P

MESH = pl.DeviceIdType.MESH
F32, BF16 = jnp.float32, jnp.bfloat16
NX, NY, NZ = 4, 8, 4
D = 4096
CAP = 8
COLS = 256
UNITS = 128
HALF = 3 * UNITS // 2
FIRST = 1408
PARTS = 4
PART = D // 2 // PARTS
CHUNKS = 3

AT_ENDS = (
    20000, 10011, 10010, 21000, 11011, 11010, 12011, 12010, 22000, 40000, 30000, 10021, 10020, 22100,
    20010, 10111, 10110, 11020, 12021, 12020, 22700, 11021, 21010, 11111, 11110, 50100, 50000, 10031,
    10030, 10121, 10120, 12031, 11031, 11030, 22200, 22600, 12030, 22010, 11121, 11120, 10130, 10131,
    10211, 10210, 11041, 12041, 20020, 22500, 10041, 11130, 21020, 22300, 10220, 60000, 11211, 11210,
    11140, 22710, 22110, 10221, 11221, 22400, 10230, 11220, 41000, 22210, 22610, 10140, 10231, 22020,
    11131, 10311, 20030, 10310, 11231, 10240, 22120, 22720, 11230, 22030, 11310, 11311, 22310, 21030,
    10321, 51100, 51000, 10320, 11321, 11320, 10331, 22510, 10330, 11331, 11240, 22220, 61000, 22730,
    22620, 11330, 10341, 11341, 22520, 22230, 22420, 22530, 22130, 22320, 22630, 22430, 22330, 22410,
)
INSIDE = (
    20000, 40000, 10011, 10010, 12010, 21000, 11011, 11010, 12011, 22000, 30000, 10021, 10020, 20010,
    10110, 20020, 10211, 10210, 11021, 10111, 11020, 12021, 12020, 22100, 22700, 21010, 11111, 11110,
    21020, 10031, 11211, 11210, 10030, 50000, 50100, 22010, 22020, 10121, 10120, 10221, 10220, 22600,
    60000, 12031, 11031, 12030, 22200, 22110, 22710, 11121, 10041, 20030, 10311, 10310, 11221, 11030,
    10130, 22720, 11220, 10131, 21030, 11311, 22210, 11310, 22120, 11120, 22030, 10230, 22610, 10231,
    12041, 22300, 22500, 11230, 10320, 22510, 22310, 11131, 22130, 22220, 10321, 22620, 11231, 10140,
    22730, 41000, 22630, 11320, 11321, 11130, 22410, 11041, 22330, 22530, 22320, 11140, 22400, 11240,
    22430, 22520, 11330, 51100, 10240, 10330, 10331, 22230, 51000, 11331, 10341, 22420, 61000, 11341,
)


def slots(routes, probs):
    n_tok = routes.shape[1]
    chosen = routes[...] == 0
    weight = jnp.sum(jnp.where(chosen, probs[...], 0.0), axis=0, keepdims=True)
    member = jnp.sum(jnp.where(chosen, 1.0, 0.0), axis=0, keepdims=True)
    weight = jnp.broadcast_to(weight, (2 * CAP, n_tok))
    member = jnp.broadcast_to(member, (2 * CAP, n_tok))
    before = lax.broadcasted_iota(jnp.int32, (n_tok, n_tok), 0)
    upto = lax.broadcasted_iota(jnp.int32, (n_tok, n_tok), 1)
    prefix = jnp.where(before <= upto, 1.0, 0.0).astype(BF16)
    position = jnp.dot(member.astype(BF16), prefix, preferred_element_type=F32)
    slot = (lax.broadcasted_iota(jnp.int32, (2 * CAP, n_tok), 0) % CAP).astype(F32)
    picker = jnp.where((position - 1.0 == slot) & (member > 0.5), 1.0, 0.0)
    return picker, jnp.sum(picker * weight, axis=1, keepdims=True)


class Sems:
    def __init__(self, send, recv):
        self.send, self.recv, self.used = send, recv, 0

    def take(self, n=1):
        at = self.used
        self.used += n
        return at


def kernel(
    tok_hbm, og_hbm, routes, probs, gu_hbm, dn_hbm,
    out_rows, out_w,
    tok, og, G, W, A_t, dH, R, yrecv, zrecv, T, crecv, xrecv, zhrecv, zhsend,
    load_sem, send_sem, recv_sem,
):
    dp, ex = lax.axis_index("dp"), lax.axis_index("expert")
    x, zh, c = dp // 4, (dp // 2) % 2, dp % 2
    zl, y = ex // NY, ex % NY

    def at(x=x, zh=zh, c=c, zl=zl, y=y):
        return ((x * 2 + zh) * 2 + c, zl * NY + y)

    right, left = at(x=(x + 1) % NX), at(x=(x + NX - 1) % NX)
    north, south = at(y=(y + 1) % NY), at(y=(y + NY - 1) % NY)
    other_core, other_run = at(c=1 - c), at(zh=1 - zh)
    in_run = [at(zl=(zl + j) % NZ) for j in range(1, NZ)]

    barrier = pltpu.get_barrier_semaphore()
    peers = [right, left, north, south, other_core, other_run] + in_run
    for peer in peers:
        pl.semaphore_signal(barrier, inc=1, device_id=peer, device_id_type=MESH)

    def cols(i):
        return pl.ds(pl.multiple_of(i * COLS, COLS), COLS)

    mine = cols(dp)
    loads = [
        pltpu.make_async_copy(tok_hbm, tok, load_sem.at[0]),
        pltpu.make_async_copy(og_hbm, og, load_sem.at[1]),
        pltpu.make_async_copy(gu_hbm.at[0], W.at[pl.ds(0, UNITS), mine], load_sem.at[2]),
        pltpu.make_async_copy(gu_hbm.at[1], W.at[pl.ds(UNITS, UNITS), mine], load_sem.at[3]),
        pltpu.make_async_copy(dn_hbm, W.at[pl.ds(2 * UNITS, UNITS), mine], load_sem.at[4]),
    ]
    for load in loads:
        load.start()

    picker, slot_weight = slots(routes, probs)
    picker_b = picker.astype(BF16)
    own_block = y * NZ + zl
    for load in loads:
        load.wait()
    x_rows = jnp.dot(picker_b, tok[...], preferred_element_type=F32)
    g_rows = jnp.dot(picker_b, og[...], preferred_element_type=F32)
    e_rows = slot_weight * g_rows
    G[own_block] = jnp.concatenate([x_rows[:CAP], e_rows[CAP:]], axis=0).astype(BF16)

    pl.semaphore_wait(barrier, len(peers))

    sems = Sems(send_sem, recv_sem)
    sent = []

    def copy(src, dst, device, k):
        return pltpu.make_async_remote_copy(
            src_ref=src,
            dst_ref=dst,
            send_sem=send_sem.at[k],
            recv_sem=recv_sem.at[k],
            device_id=device,
            device_id_type=MESH,
        )

    def go(src, dst, device, k=None):
        one = copy(src, dst, device, sems.take() if k is None else k)
        one.start()
        sent.append(one)
        return one

    upper = zl // 2
    m = zl * (1 - upper) + (3 - zl) * upper
    order = [b * (1 - upper) + (3 - b) * upper for b in (m, 1 - m, 2, 3)]

    col_parts = [pl.ds(0, FIRST), pl.ds(FIRST, FIRST), pl.ds(2 * FIRST, D - 2 * FIRST)]
    held = {}

    def sem_of(key, n=1):
        if key not in held:
            held[key] = sems.take(n)
        return held[key]

    def z_copy(part, d, zs, up):
        ref = G.at[(y + d) % NY * NZ + zs, :, col_parts[part]]
        to_send = sem_of(("up" if up else "down", part, d), NZ)
        return pltpu.make_async_remote_copy(
            src_ref=ref,
            dst_ref=ref,
            send_sem=send_sem.at[to_send + zs],
            recv_sem=recv_sem.at[sem_of(("up", part, d), NZ) + zs],
            device_id=at(zl=(zl + (1 if up else NZ - 1)) % NZ),
            device_id_type=MESH,
        )

    def z_both(act, part, d, zs):
        @pl.when((zs <= zl) & (zl < NZ - 1))
        def _():
            act(z_copy(part, d, zs, True))

        @pl.when((zs >= zl) & (zl > 0))
        def _():
            act(z_copy(part, d, zs, False))

    def start(one):
        one.start()

    def hops(k, plus):
        return 4 if (k in (0, 3)) == plus else 3

    def y_copy(part, k, h, plus):
        src_y = (y + (NY - h + 1 if plus else h - 1)) % NY
        ref = G.at[src_y * NZ + order[k], :, col_parts[part]]
        return copy(ref, ref, north if plus else south, sem_of(("y", part, k, h, plus)))

    def block_of(xx, zz, cc):
        return (xx * 2 + zz) * 2 + cc

    def w_ref(xx, zz, rows=pl.ds(0, 3 * UNITS), cc=c):
        return W.at[rows, cols(block_of(xx, zz, cc))]

    lo, hi = pl.ds(0, HALF), pl.ds(HALF, HALF)
    x1, x2, x3 = (x + 1) % NX, (x + 2) % NX, (x + 3) % NX
    runs = (zh, 1 - zh)

    def to_core(n, xx):
        ref = w_ref(xx, runs[n])
        return copy(ref, ref, other_core, sem_of(("core", n, [xx is one for one in (x, x1, x2, x3)].index(True))))

    def to_run():
        return copy(w_ref(x, zh), w_ref(x, zh), other_run, sem_of("run"))

    def x_copy(n, hop, plus):
        if hop == 1:
            ref = w_ref(x, runs[n])
        else:
            ref = w_ref(x3, runs[n], lo) if plus else w_ref(x1, runs[n], hi)
        return copy(ref, ref, right if plus else left, sem_of(("x", n, hop, plus)))

    y_keys = [(p, k, h, plus) for p in range(3) for k in range(4 if p < 2 else 1) for plus in (True, False) for h in range(1, hops(k, plus) + 1)]
    z_keys = [(p, d, k) for p in range(3) for d in range(1 if p < 2 else NY) for k in range(4)]
    x_keys = [(n, hop, plus) for n in range(2) for hop in (1, 2) for plus in (True, False)]
    core_keys = [(n, xx) for n in range(2) for xx in (x, x1, x2, x3)]

    def exchange(codes):
        taken = set()

        def take(one, *key):
            if key not in taken:
                taken.add(key)
                one().wait_recv()

        def take_y(*key):
            take(lambda: y_copy(*key), "y", *key)

        def take_z(p, d, k):
            take(lambda: z_copy(p, d, order[k], True), "z", p, d, k)

        for code in codes:
            kind, p, q, r, w = (code // 10**e % 10 for e in (4, 3, 2, 1, 0))
            if kind == 1:
                if r > 1:
                    take_y(p, q, r - 1, w == 1)
                elif q > 0:
                    take_z(p, 0, q)
                y_copy(p, q, r, w == 1).start()
            elif kind == 2:
                if r > 0:
                    take_z(p, q, r)
                elif q > 0:
                    take_y(p, 0, min(q, NY - q), q >= 4)
                z_both(start, p, q, order[r])
            elif kind == 3:
                to_run().start()
            elif kind == 4:
                if p == 1:
                    to_run().wait_recv()
                x_copy(p, 1, True).start()
                x_copy(p, 1, False).start()
                to_core(p, x).start()
            elif kind == 5:
                x_copy(p, 1, q == 1).wait_recv()
                x_copy(p, 2, q == 1).start()
                to_core(p, x3 if q == 1 else x1).start()
            else:
                x_copy(p, 2, True).wait_recv()
                x_copy(p, 2, False).wait_recv()
                to_core(p, x2).start()
        for key in y_keys:
            take_y(*key)
        for key in core_keys:
            to_core(*key).wait_recv()

    for key in y_keys:
        sem_of(("y", *key))

    @pl.when((zl == 0) | (zl == NZ - 1))
    def _():
        exchange(AT_ENDS)

    @pl.when((zl > 0) & (zl < NZ - 1))
    def _():
        exchange(INSIDE)

    for half in range(2):
        g = G[pl.ds(half * 16, 16)].reshape(256, D)
        pre = lax.dot_general(g, W[...], (((1,), (1,)), ((), ())), preferred_element_type=F32)
        pre = pre.reshape(16, 2 * CAP, 3 * UNITS)
        gate_pre = pre[:, :CAP, :UNITS]
        up_pre = pre[:, :CAP, UNITS : 2 * UNITS]
        hidden_grad = pre[:, CAP:, 2 * UNITS :]
        sig = 1.0 / (1.0 + jnp.exp(-gate_pre))
        activated = gate_pre * sig
        hidden = activated * up_pre
        up_grad = hidden_grad * activated
        gate_grad = hidden_grad * up_pre * sig * (1.0 + gate_pre * (1.0 - sig))
        zero = jnp.zeros_like(hidden)
        a = jnp.concatenate(
            [
                jnp.concatenate([gate_grad, up_grad, zero], axis=2),
                jnp.concatenate([zero, zero, hidden], axis=2),
            ],
            axis=1,
        ).reshape(256, 3 * UNITS)
        A_t[:, pl.ds(half * 256, 256)] = a.T.astype(BF16)
        grads = jnp.concatenate([gate_grad, up_grad], axis=2).reshape(128, 2 * UNITS)
        dH[pl.ds(half * 128, 128)] = grads.astype(BF16)

    def weight_grad(i):
        g = G[:, :, cols(i)].reshape(512, COLS)
        T[i] = jnp.dot(A_t[...], g, preferred_element_type=F32).astype(BF16)

    x_order = [x2, x1, x3, x]
    core_copies = []
    for n, xx in enumerate(x_order):
        for zz in range(2):
            i = block_of(xx, zz, 1 - c)
            weight_grad(i)
            core_copies.append(go(T.at[i], crecv.at[2 * n + zz], other_core))

    def r_part(yy, p):
        return R.at[yy, :, :, pl.ds(p * PART, PART)]

    def r_hops(p, plus):
        return 4 if (p % 2 == 0) == plus else 3

    r_slot = {}
    for plus in (True, False):
        for p in range(PARTS):
            for s in range(1, r_hops(p, plus) + 1):
                r_slot[p, s, plus] = len(r_slot)
    r_live = {}

    def r_dest(p, s, plus):
        d = r_hops(p, plus) - s + 1
        return (y + (d if plus else NY - d)) % NY

    def r_send(p, s, plus):
        r_live[p, s, plus] = go(
            r_part(r_dest(p, s, plus), p),
            yrecv.at[r_slot[p, s, plus]],
            north if plus else south,
        )

    def r_step(p, s, plus):
        r_live[p, s, plus].wait_recv()
        dest = r_dest(p, s + 1, plus)
        ref = r_part(dest, p)
        total = ref[...].astype(F32) + yrecv[r_slot[p, s, plus]].astype(F32)
        ref[...] = total.astype(BF16)
        r_send(p, s + 1, plus)

    def r_steps(s, parts):
        for p in parts:
            for plus in (True, False):
                if s < r_hops(p, plus):
                    r_step(p, s, plus)

    for p in range(PARTS):
        parts = []
        for base in (0, D // 2):
            w = W[pl.ds(0, 2 * UNITS), pl.ds(base + p * PART, PART)]
            part = jnp.dot(dH[...], w, preferred_element_type=F32)
            parts.append(part.reshape(NY * NZ, CAP, PART))
        both = jnp.concatenate(parts, axis=1).astype(BF16)
        R[:, :, :, pl.ds(p * PART, PART)] = both.reshape(NY, NZ, 2 * CAP, PART)
        for plus in (True, False):
            r_send(p, 1, plus)

    for n, xx in enumerate(x_order):
        for zz in range(2):
            weight_grad(block_of(xx, zz, c))

    def core_sum(n, zz):
        core_copies[2 * n + zz].wait_recv()
        i = block_of(x_order[n], zz, c)
        T[i] = (T[i].astype(F32) + crecv[2 * n + zz].astype(F32)).astype(BF16)

    CH = 3 * UNITS // CHUNKS

    def t_ref(xx, zz, q):
        return T.at[block_of(xx, zz, c), pl.ds(q * CH, CH)]

    def x_ref(slot, q):
        return xrecv.at[slot, pl.ds(q * CH, CH)]

    chunks = range(CHUNKS)
    xp1, xm1, xp2, xm2, xp3, xm3 = {}, {}, {}, {}, {}, {}
    core_sum(0, 0)
    core_sum(0, 1)
    for q in chunks:
        xp1[q] = go(t_ref(x2, 0, q), x_ref(0, q), right)
        xm1[q] = go(t_ref(x2, 1, q), x_ref(1, q), left)
    core_sum(1, 1)
    core_sum(2, 0)
    for q in chunks:
        xp2[q] = go(t_ref(x1, 1, q), x_ref(2, q), right)
        xm2[q] = go(t_ref(x3, 0, q), x_ref(3, q), left)
    core_sum(1, 0)
    core_sum(2, 1)
    core_sum(3, 0)
    core_sum(3, 1)

    def x_turn(q):
        for live, slot, xx, zz in ((xp1, 0, x1, 0), (xm1, 1, x3, 1)):
            live[q].wait_recv()
            ref = t_ref(xx, zz, q)
            ref[...] = (ref[...].astype(F32) + x_ref(slot, q)[...].astype(F32)).astype(BF16)
        xp3[q] = go(t_ref(x1, 0, q), x_ref(4, q), right)
        xm3[q] = go(t_ref(x3, 1, q), x_ref(5, q), left)

    zh_copy = {}

    def x_end(q):
        for live in (xp2, xm2, xp3, xm3):
            live[q].wait_recv()
        rows = pl.ds(q * CH, CH)
        total = t_ref(x, 1 - zh, q)[...].astype(F32)
        total = total + xrecv[4 - 2 * (1 - zh), rows].astype(F32)
        total = total + xrecv[3 + 2 * (1 - zh), rows].astype(F32)
        zhsend[rows] = total.astype(BF16)
        zh_copy[q] = go(zhsend.at[rows], zhrecv.at[rows], other_run)

    z_live = {}

    def r_end(p):
        for plus in (True, False):
            r_live[p, r_hops(p, plus), plus].wait_recv()
        ref = r_part(y, p)
        total = ref[...].astype(F32)
        for plus in (True, False):
            total = total + yrecv[r_slot[p, r_hops(p, plus), plus]].astype(F32)
        ref[...] = total.astype(BF16)
        base = sems.take(NZ)
        for j in range(1, NZ):
            zs = (zl + j) % NZ
            one = pltpu.make_async_remote_copy(
                src_ref=R.at[y, zs, :, pl.ds(p * PART, PART)],
                dst_ref=zrecv.at[p, zl],
                send_sem=send_sem.at[base + zs],
                recv_sem=recv_sem.at[base + zl],
                device_id=at(zl=zs),
                device_id_type=MESH,
            )
            one.start()
            sent.append(one)
        z_live[p] = base

    all_parts = range(PARTS)
    r_steps(1, all_parts)
    for q in chunks:
        x_turn(q)
    r_steps(2, all_parts)
    for q in chunks:
        x_end(q)
    r_steps(3, all_parts)
    for p in all_parts:
        r_end(p)

    for q in chunks:
        rows = pl.ds(q * CH, CH)
        total = t_ref(x, zh, q)[...].astype(F32)
        total = total + xrecv[4 - 2 * zh, rows].astype(F32) + xrecv[3 + 2 * zh, rows].astype(F32)
        zh_copy[q].wait_recv()
        out_w[rows] = total + zhrecv[rows].astype(F32)

    for p in all_parts:
        total = R[y, zl, :, pl.ds(p * PART, PART)].astype(F32)
        for j in range(1, NZ):
            zs = (zl + j) % NZ
            pltpu.make_async_remote_copy(
                src_ref=zrecv.at[p, zs],
                dst_ref=zrecv.at[p, zs],
                send_sem=send_sem.at[z_live[p] + zs],
                recv_sem=recv_sem.at[z_live[p] + zs],
                device_id=at(zl=zs),
                device_id_type=MESH,
            ).wait_recv()
            total = total + zrecv[p, zs].astype(F32)
        out_rows[:, pl.ds(p * PART, PART)] = total.astype(BF16)

    for one in sent:
        one.wait_send()
    for key in y_keys:
        y_copy(*key).wait_send()
    for p, d, k in z_keys:
        z_both(lambda one: one.wait_send(), p, d, order[k])
    for key in x_keys:
        x_copy(*key).wait_send()
    for key in core_keys:
        to_core(*key).wait_send()
    to_run().wait_send()


def finish(routes, probs, rows_hbm, grads_hbm, out_tok, out_gu, out_dn, rows, grads, buf, sem):
    copies = [
        pltpu.make_async_copy(grads.at[pl.ds(0, UNITS)], out_gu.at[0], sem.at[0]),
        pltpu.make_async_copy(grads.at[pl.ds(UNITS, UNITS)], out_gu.at[1], sem.at[1]),
        pltpu.make_async_copy(grads.at[pl.ds(2 * UNITS, UNITS)], out_dn, sem.at[2]),
    ]
    loads = [
        pltpu.make_async_copy(rows_hbm, rows, sem.at[5]),
        pltpu.make_async_copy(grads_hbm, grads, sem.at[6]),
    ]
    for load in loads:
        load.start()
    n_tok = out_tok.shape[0]
    picker, _ = slots(routes, probs)
    placed = jnp.concatenate([picker, jnp.zeros((n_tok - 2 * CAP, n_tok), F32)], axis=0).T
    placed = placed[:, : 2 * CAP]
    lane = lax.broadcasted_iota(jnp.int32, (n_tok, 2 * CAP), 1)
    low = jnp.where(lane < CAP, placed, 0.0).astype(BF16)
    high = jnp.where(lane >= CAP, placed, 0.0).astype(BF16)
    loads[1].wait()
    for one in copies:
        one.start()
    loads[0].wait()
    for n, part in enumerate((low, high)):
        at = pl.ds(n * (D // 2), D // 2)
        buf[:, at] = jnp.dot(part, rows[...], preferred_element_type=F32).astype(BF16)
        one = pltpu.make_async_copy(buf.at[:, at], out_tok.at[:, at], sem.at[3 + n])
        one.start()
        copies.append(one)
    for one in copies:
        one.wait()


def on_device(tokens_in, out_grad, routes, router_probs, gate_up, down_proj):
    vmem = pl.BlockSpec(memory_space=pltpu.VMEM)
    hbm = pl.BlockSpec(memory_space=pltpu.HBM)
    n_tok = tokens_in.shape[0]
    blocks = NY * NZ
    n_sems = 320
    routes, router_probs = routes.T, router_probs.T
    rows, grads = pl.pallas_call(
        kernel,
        out_shape=(
            jax.ShapeDtypeStruct((2 * CAP, D // 2), BF16),
            jax.ShapeDtypeStruct((3 * UNITS, COLS), F32),
        ),
        in_specs=[hbm, hbm, vmem, vmem, hbm, hbm],
        out_specs=(vmem, vmem),
        scratch_shapes=[
            pltpu.VMEM((n_tok, D), BF16),
            pltpu.VMEM((n_tok, D), BF16),
            pltpu.VMEM((blocks, 2 * CAP, D), BF16),
            pltpu.VMEM((3 * UNITS, D), BF16),
            pltpu.VMEM((3 * UNITS, 2 * CAP * blocks), BF16),
            pltpu.VMEM((CAP * blocks, 2 * UNITS), BF16),
            pltpu.VMEM((NY, NZ, 2 * CAP, D // 2), BF16),
            pltpu.VMEM((7 * PARTS, NZ, 2 * CAP, PART), BF16),
            pltpu.VMEM((PARTS, NZ, 2 * CAP, PART), BF16),
            pltpu.VMEM((16, 3 * UNITS, COLS), BF16),
            pltpu.VMEM((8, 3 * UNITS, COLS), BF16),
            pltpu.VMEM((6, 3 * UNITS, COLS), BF16),
            pltpu.VMEM((3 * UNITS, COLS), BF16),
            pltpu.VMEM((3 * UNITS, COLS), BF16),
            pltpu.SemaphoreType.DMA((5,)),
            pltpu.SemaphoreType.DMA((n_sems,)),
            pltpu.SemaphoreType.DMA((n_sems,)),
        ],
        compiler_params=pltpu.CompilerParams(
            collective_id=0, has_side_effects=True, vmem_limit_bytes=56 * 2**20
        ),
        cost_estimate=pl.CostEstimate(
            flops=6 * 10**9, bytes_accessed=4 * 2**20, transcendentals=2**15
        ),
        name="expert_backward",
    )(tokens_in, out_grad, routes, router_probs, gate_up, down_proj)
    return pl.pallas_call(
        finish,
        out_shape=(
            jax.ShapeDtypeStruct(tokens_in.shape, BF16),
            jax.ShapeDtypeStruct(gate_up.shape, F32),
            jax.ShapeDtypeStruct(down_proj.shape, F32),
        ),
        in_specs=[vmem, vmem, hbm, hbm],
        out_specs=(hbm, hbm, hbm),
        scratch_shapes=[
            pltpu.VMEM((2 * CAP, D // 2), BF16),
            pltpu.VMEM((3 * UNITS, COLS), F32),
            pltpu.VMEM((n_tok, D), BF16),
            pltpu.SemaphoreType.DMA((7,)),
        ],
        name="finish",
    )(routes, router_probs, rows, grads)


def solution(mesh):
    in_specs = (
        P(("dp", "expert"), None),
        P(("dp", "expert"), None),
        P(("dp", "expert"), None),
        P(("dp", "expert"), None),
        P(None, "expert", "dp"),
        P("expert", "dp"),
    )
    out_specs = (P(("dp", "expert"), None), P(None, "expert", "dp"), P("expert", "dp"))
    return jax.shard_map(
        on_device, mesh=mesh, in_specs=in_specs, out_specs=out_specs, check_vma=False
    )
```

```python
import jax
import jax.numpy as jnp
from jax import lax
from jax.experimental import pallas as pl
from jax.experimental.pallas import tpu as pltpu
from jax.sharding import PartitionSpec as P

MESH = pl.DeviceIdType.MESH
F32, BF16 = jnp.float32, jnp.bfloat16
NX, NY, NZ = 4, 8, 4
D = 4096
CAP = 8
COLS = 256
UNITS = 128
HALF = 3 * UNITS // 2
FIRST = 1408
PARTS = 4
PART = D // 2 // PARTS
CHUNKS = 2
X_ROWS = 256
CH = X_ROWS // CHUNKS
Z_ROWS = 3 * UNITS - X_ROWS

AFTER = (
    10010, 11000, 10000, 12100, 11100, 10100, 12010, 10110, 11200, 12310, 12300, 12110, 12000, 10210,
    10200, 13010, 14100, 13000, 22000, 14010, 11300, 14110, 14000, 12210, 13110, 10310, 13100, 22100,
    19010, 10300, 19011, 12200, 13200, 13210, 15010, 22200, 15100, 19110, 19111, 19211, 15110, 19210,
    16000, 16010, 15000, 19310, 19021, 19311, 16100, 13310, 19020, 16110, 13300, 22300, 23000, 19120,
    19221, 19121, 24000, 24100, 19220, 17000, 19320, 17100, 23100, 19031, 19130, 26100, 19321, 23200,
    25100, 26000, 19231, 19330, 20000, 25000, 20100, 20200, 23300, 20300, 21100, 18100, 18000, 27000,
    21000, 21200, 21300,
)
AT_ENDS = (
    11010, 21000, 11011, 20000, 12010, 10011, 10010, 12011, 40000, 30000, 11111, 11110, 11021, 11020,
    22100, 10111, 10110, 12021, 12020, 10021, 10020, 22000, 21010, 11121, 11120, 20010, 50000, 11031,
    11030, 10121, 50100, 22600, 22200, 10120, 12031, 12030, 10031, 22700, 10030, 11130, 21020, 11211,
    11210, 22110, 11041, 20020, 10211, 11131, 10210, 60000, 22010, 41000, 10130, 22500, 12041, 10041,
    11140, 10131, 22300, 11220, 10220, 11221, 10140, 22710, 11311, 22210, 11310, 22400, 11230, 10311,
    20030, 10221, 21030, 10310, 22020, 22120, 22720, 22610, 22220, 11231, 11321, 10230, 10321, 51100,
    11320, 11240, 51000, 10231, 10240, 10320, 11331, 22310, 22030, 22620, 10331, 61000, 11330, 11341,
    22530, 22510, 22130, 10341, 10330, 22430, 22630, 22320, 22420, 22730, 22230, 22330, 22410, 22520,
)
INSIDE = (
    21000, 11011, 11010, 20000, 12011, 12010, 10011, 10010, 40000, 11210, 11021, 30000, 21020, 21010,
    11211, 11111, 20010, 20020, 11110, 10021, 11020, 10211, 10111, 10110, 10210, 22100, 22000, 22700,
    11220, 12020, 50100, 50000, 12021, 11221, 11120, 11031, 11121, 11030, 12031, 22200, 21030, 10020,
    10221, 10120, 11311, 22600, 11310, 10220, 10311, 22020, 10031, 10121, 60000, 10310, 11231, 11130,
    22110, 20030, 22710, 11131, 22610, 22220, 12030, 22720, 22010, 11041, 22120, 10030, 22310, 11230,
    22620, 11320, 10231, 22210, 11321, 22510, 41000, 12041, 22500, 10131, 22130, 10041, 22300, 10230,
    10320, 22030, 22730, 11140, 10321, 22410, 22530, 10130, 22320, 51000, 22230, 11330, 10330, 11240,
    51100, 11331, 22520, 22330, 10140, 22400, 10331, 22630, 10240, 11341, 22430, 61000, 10341, 22420,
)


def slots(routes, probs):
    n_tok = routes.shape[1]
    chosen = routes[...] == 0
    weight = jnp.sum(jnp.where(chosen, probs[...], 0.0), axis=0, keepdims=True)
    member = jnp.sum(jnp.where(chosen, 1.0, 0.0), axis=0, keepdims=True)
    weight = jnp.broadcast_to(weight, (2 * CAP, n_tok))
    member = jnp.broadcast_to(member, (2 * CAP, n_tok))
    before = lax.broadcasted_iota(jnp.int32, (n_tok, n_tok), 0)
    upto = lax.broadcasted_iota(jnp.int32, (n_tok, n_tok), 1)
    prefix = jnp.where(before <= upto, 1.0, 0.0).astype(BF16)
    position = jnp.dot(member.astype(BF16), prefix, preferred_element_type=F32)
    slot = (lax.broadcasted_iota(jnp.int32, (2 * CAP, n_tok), 0) % CAP).astype(F32)
    picker = jnp.where((position - 1.0 == slot) & (member > 0.5), 1.0, 0.0)
    return picker, jnp.sum(picker * weight, axis=1, keepdims=True)


class Sems:
    def __init__(self, send, recv):
        self.send, self.recv, self.used = send, recv, 0

    def take(self, n=1):
        at = self.used
        self.used += n
        return at


def kernel(
    tok_hbm, og_hbm, routes_hbm, probs_hbm, gu_hbm, dn_hbm,
    rows_hbm, w_hbm,
    routes, probs, out_rows, out_w, tok, og, G, W, A_t, dH, R, yrecv, zrecv, T, crecv, xrecv, zhrecv, zhsend, zwrecv, hrecv,
    load_sem, send_sem, recv_sem,
):
    dp, ex = lax.axis_index("dp"), lax.axis_index("expert")
    x, zh, c = dp // 4, (dp // 2) % 2, dp % 2
    zl, y = ex // NY, ex % NY

    def at(x=x, zh=zh, c=c, zl=zl, y=y):
        return ((x * 2 + zh) * 2 + c, zl * NY + y)

    right, left = at(x=(x + 1) % NX), at(x=(x + NX - 1) % NX)
    north, south = at(y=(y + 1) % NY), at(y=(y + NY - 1) % NY)
    other_core, other_run = at(c=1 - c), at(zh=1 - zh)
    in_run = [at(zl=(zl + j) % NZ) for j in range(1, NZ)]

    barrier = pltpu.get_barrier_semaphore()
    peers = [right, left, north, south, other_core, other_run] + in_run
    for peer in peers:
        pl.semaphore_signal(barrier, inc=1, device_id=peer, device_id_type=MESH)

    def cols(i):
        return pl.ds(pl.multiple_of(i * COLS, COLS), COLS)

    mine = cols(dp)
    routing = [
        pltpu.make_async_copy(routes_hbm, routes, load_sem.at[5]),
        pltpu.make_async_copy(probs_hbm, probs, load_sem.at[6]),
    ]
    loads = [
        pltpu.make_async_copy(tok_hbm, tok, load_sem.at[0]),
        pltpu.make_async_copy(og_hbm, og, load_sem.at[1]),
        pltpu.make_async_copy(gu_hbm.at[0], W.at[pl.ds(0, UNITS), mine], load_sem.at[2]),
        pltpu.make_async_copy(gu_hbm.at[1], W.at[pl.ds(UNITS, UNITS), mine], load_sem.at[3]),
        pltpu.make_async_copy(dn_hbm, W.at[pl.ds(2 * UNITS, UNITS), mine], load_sem.at[4]),
    ]
    for load in routing + loads:
        load.start()
    for load in routing:
        load.wait()

    picker, slot_weight = slots(routes, probs)
    picker_b = picker.astype(BF16)
    own_block = y * NZ + zl
    for load in loads:
        load.wait()
    x_rows = jnp.dot(picker_b, tok[...], preferred_element_type=F32)
    g_rows = jnp.dot(picker_b, og[...], preferred_element_type=F32)
    e_rows = slot_weight * g_rows
    G[own_block] = jnp.concatenate([x_rows[:CAP], e_rows[CAP:]], axis=0).astype(BF16)

    pl.semaphore_wait(barrier, len(peers))

    sems = Sems(send_sem, recv_sem)
    sent = []

    def copy(src, dst, device, k):
        return pltpu.make_async_remote_copy(
            src_ref=src,
            dst_ref=dst,
            send_sem=send_sem.at[k],
            recv_sem=recv_sem.at[k],
            device_id=device,
            device_id_type=MESH,
        )

    def go(src, dst, device, k=None):
        one = copy(src, dst, device, sems.take() if k is None else k)
        one.start()
        sent.append(one)
        return one

    upper = zl // 2
    m = zl * (1 - upper) + (3 - zl) * upper
    order = [b * (1 - upper) + (3 - b) * upper for b in (m, 1 - m, 2, 3)]

    col_parts = [pl.ds(0, FIRST), pl.ds(FIRST, FIRST), pl.ds(2 * FIRST, D - 2 * FIRST)]
    held = {}

    def sem_of(key, n=1):
        if key not in held:
            held[key] = sems.take(n)
        return held[key]

    def z_copy(part, d, zs, up):
        ref = G.at[(y + d) % NY * NZ + zs, :, col_parts[part]]
        to_send = sem_of(("up" if up else "down", part, d), NZ)
        return pltpu.make_async_remote_copy(
            src_ref=ref,
            dst_ref=ref,
            send_sem=send_sem.at[to_send + zs],
            recv_sem=recv_sem.at[sem_of(("up", part, d), NZ) + zs],
            device_id=at(zl=(zl + (1 if up else NZ - 1)) % NZ),
            device_id_type=MESH,
        )

    def z_both(act, part, d, zs):
        @pl.when((zs <= zl) & (zl < NZ - 1))
        def _():
            act(z_copy(part, d, zs, True))

        @pl.when((zs >= zl) & (zl > 0))
        def _():
            act(z_copy(part, d, zs, False))

    def start(one):
        one.start()

    def hops(k, plus):
        return 4 if (k in (0, 3)) == plus else 3

    def y_copy(part, k, h, plus):
        src_y = (y + (NY - h + 1 if plus else h - 1)) % NY
        ref = G.at[src_y * NZ + order[k], :, col_parts[part]]
        return copy(ref, ref, north if plus else south, sem_of(("y", part, k, h, plus)))

    def block_of(xx, zz, cc):
        return (xx * 2 + zz) * 2 + cc

    def w_ref(xx, zz, rows=pl.ds(0, 3 * UNITS), cc=c):
        return W.at[rows, cols(block_of(xx, zz, cc))]

    lo, hi = pl.ds(0, HALF), pl.ds(HALF, HALF)
    x1, x2, x3 = (x + 1) % NX, (x + 2) % NX, (x + 3) % NX
    runs = (zh, 1 - zh)

    def to_core(n, xx):
        ref = w_ref(xx, runs[n])
        return copy(ref, ref, other_core, sem_of(("core", n, [xx is one for one in (x, x1, x2, x3)].index(True))))

    def to_run():
        return copy(w_ref(x, zh), w_ref(x, zh), other_run, sem_of("run"))

    def x_copy(n, hop, plus):
        if hop == 1:
            ref = w_ref(x, runs[n])
        else:
            ref = w_ref(x3, runs[n], lo) if plus else w_ref(x1, runs[n], hi)
        return copy(ref, ref, right if plus else left, sem_of(("x", n, hop, plus)))

    y_keys = [(p, k, h, plus) for p in range(3) for k in range(4 if p < 2 else 1) for plus in (True, False) for h in range(1, hops(k, plus) + 1)]
    z_keys = [(p, d, k) for p in range(3) for d in range(1 if p < 2 else NY) for k in range(4)]
    x_keys = [(n, hop, plus) for n in range(2) for hop in (1, 2) for plus in (True, False)]
    core_keys = [(n, xx) for n in range(2) for xx in (x, x1, x2, x3)]

    def exchange(codes):
        taken = set()

        def take(one, *key):
            if key not in taken:
                taken.add(key)
                one().wait_recv()

        def take_y(*key):
            take(lambda: y_copy(*key), "y", *key)

        def take_z(p, d, k):
            take(lambda: z_copy(p, d, order[k], True), "z", p, d, k)

        for code in codes:
            kind, p, q, r, w = (code // 10**e % 10 for e in (4, 3, 2, 1, 0))
            if kind == 1:
                if r > 1:
                    take_y(p, q, r - 1, w == 1)
                elif q > 0:
                    take_z(p, 0, q)
                y_copy(p, q, r, w == 1).start()
            elif kind == 2:
                if r > 0:
                    take_z(p, q, r)
                elif q > 0:
                    take_y(p, 0, min(q, NY - q), q >= 4)
                z_both(start, p, q, order[r])
            elif kind == 3:
                to_run().start()
            elif kind == 4:
                if p == 1:
                    to_run().wait_recv()
                x_copy(p, 1, True).start()
                x_copy(p, 1, False).start()
                to_core(p, x).start()
            elif kind == 5:
                x_copy(p, 1, q == 1).wait_recv()
                x_copy(p, 2, q == 1).start()
                to_core(p, x3 if q == 1 else x1).start()
            else:
                x_copy(p, 2, True).wait_recv()
                x_copy(p, 2, False).wait_recv()
                to_core(p, x2).start()
        for key in y_keys:
            take_y(*key)
        for key in core_keys:
            to_core(*key).wait_recv()

    for key in y_keys:
        sem_of(("y", *key))

    @pl.when((zl == 0) | (zl == NZ - 1))
    def _():
        exchange(AT_ENDS)

    @pl.when((zl > 0) & (zl < NZ - 1))
    def _():
        exchange(INSIDE)

    for half in range(2):
        g = G[pl.ds(half * 16, 16)].reshape(256, D)
        pre = lax.dot_general(g, W[...], (((1,), (1,)), ((), ())), preferred_element_type=F32)
        pre = pre.reshape(16, 2 * CAP, 3 * UNITS)
        gate_pre = pre[:, :CAP, :UNITS]
        up_pre = pre[:, :CAP, UNITS : 2 * UNITS]
        hidden_grad = pre[:, CAP:, 2 * UNITS :]
        sig = 1.0 / (1.0 + jnp.exp(-gate_pre))
        activated = gate_pre * sig
        hidden = activated * up_pre
        up_grad = hidden_grad * activated
        gate_grad = hidden_grad * up_pre * sig * (1.0 + gate_pre * (1.0 - sig))
        zero = jnp.zeros_like(hidden)
        a = jnp.concatenate(
            [
                jnp.concatenate([gate_grad, up_grad, zero], axis=2),
                jnp.concatenate([zero, zero, hidden], axis=2),
            ],
            axis=1,
        ).reshape(256, 3 * UNITS)
        A_t[:, pl.ds(half * 256, 256)] = a.T.astype(BF16)
        grads = jnp.concatenate([gate_grad, up_grad], axis=2).reshape(128, 2 * UNITS)
        dH[pl.ds(half * 128, 128)] = grads.astype(BF16)

    def weight_grad(i):
        g = G[:, :, cols(i)].reshape(512, COLS)
        T[i] = jnp.dot(A_t[...], g, preferred_element_type=F32).astype(BF16)

    written = []
    x_order = [x2, x1, x3, x]

    def begin(one):
        one.start()
        sent.append(one)

    def add(ref, *terms):
        total = ref[...].astype(F32)
        for term in terms:
            total = total + term.astype(F32)
        return total

    def core_copy(n, zz):
        i = block_of(x_order[n], zz, 1 - c)
        return copy(T.at[i], crecv.at[2 * n + zz], other_core, sem_of(("c", n, zz)))

    def core_sum(n, zz):
        core_copy(n, zz).wait_recv()
        ref = T.at[block_of(x_order[n], zz, c)]
        ref[...] = add(ref, crecv[2 * n + zz]).astype(BF16)

    def r_part(yy, p):
        return R.at[yy, :, :, pl.ds(p * PART, PART)]

    def r_hops(p, plus):
        return 4 if (p % 2 == 0) == plus else 3

    r_slot = {}
    for plus in (True, False):
        for p in range(PARTS):
            for s in range(1, r_hops(p, plus) + 1):
                r_slot[p, s, plus] = len(r_slot)

    def r_dest(p, s, plus):
        d = r_hops(p, plus) - s + 1
        return (y + (d if plus else NY - d)) % NY

    def r_copy(p, s, plus):
        src, dst = r_part(r_dest(p, s, plus), p), yrecv.at[r_slot[p, s, plus]]
        return copy(src, dst, north if plus else south, sem_of(("r", p, s, plus)))

    def r_step(p, s, plus):
        r_copy(p, s, plus).wait_recv()
        ref = r_part(r_dest(p, s + 1, plus), p)
        ref[...] = add(ref, yrecv[r_slot[p, s, plus]]).astype(BF16)
        begin(r_copy(p, s + 1, plus))

    def row_grad(p):
        parts = []
        for base in (0, D // 2):
            w = W[pl.ds(0, 2 * UNITS), pl.ds(base + p * PART, PART)]
            part = jnp.dot(dH[...], w, preferred_element_type=F32)
            parts.append(part.reshape(NY * NZ, CAP, PART))
        both = jnp.concatenate(parts, axis=1).astype(BF16)
        R[:, :, :, pl.ds(p * PART, PART)] = both.reshape(NY, NZ, 2 * CAP, PART)
        for plus in (True, False):
            begin(r_copy(p, 1, plus))

    def run_copy(p, zs, arriving):
        base = sem_of(("run", p), NZ)
        return pltpu.make_async_remote_copy(
            src_ref=R.at[y, zs, :, pl.ds(p * PART, PART)],
            dst_ref=zrecv.at[p, zs if arriving else zl],
            send_sem=send_sem.at[base + zs],
            recv_sem=recv_sem.at[base + (zs if arriving else zl)],
            device_id=at(zl=zs),
            device_id_type=MESH,
        )

    def r_end(p):
        ways = (True, False)
        for plus in ways:
            r_copy(p, r_hops(p, plus), plus).wait_recv()
        ref = r_part(y, p)
        terms = [yrecv[r_slot[p, r_hops(p, plus), plus]] for plus in ways]
        ref[...] = add(ref, *terms).astype(BF16)
        for j in range(1, NZ):
            begin(run_copy(p, (zl + j) % NZ, False))

    def r_final(p):
        others = [(zl + j) % NZ for j in range(1, NZ)]
        for zs in others:
            run_copy(p, zs, True).wait_recv()
        here = pl.ds(p * PART, PART)
        total = add(R.at[y, zl, :, here], *[zrecv[p, zs] for zs in others])
        out_rows[:, here] = total.astype(BF16)

    def t_ref(xx, zz, rows):
        return T.at[block_of(xx, zz, c), rows]

    def x_rows_of(q):
        return pl.ds(q * CH, CH)

    def t_copy(step, q, plus):
        xx, zz = {
            (1, True): (x2, 0), (1, False): (x2, 1), (2, True): (x1, 1),
            (2, False): (x3, 0), (3, True): (x1, 0), (3, False): (x3, 1),
        }[step, plus]
        slot = 2 * (step - 1) + (0 if plus else 1)
        src, dst = t_ref(xx, zz, x_rows_of(q)), xrecv.at[slot, x_rows_of(q)]
        return copy(src, dst, right if plus else left, sem_of(("t", step, q, plus)))

    def x_turn(q, plus):
        t_copy(1, q, plus).wait_recv()
        ref = t_ref(x1, 0, x_rows_of(q)) if plus else t_ref(x3, 1, x_rows_of(q))
        ref[...] = add(ref, xrecv[0 if plus else 1, x_rows_of(q)]).astype(BF16)
        begin(t_copy(3, q, plus))

    def x_total(zz, rows):
        return add(t_ref(x, zz, rows), xrecv[4 - 2 * zz, rows], xrecv[3 + 2 * zz, rows])

    def zh_copy(q):
        rows = x_rows_of(q)
        return copy(zhsend.at[rows], zhrecv.at[rows], other_run, sem_of(("zh", q)))

    def x_end(q):
        for step in (2, 3):
            for plus in (True, False):
                t_copy(step, q, plus).wait_recv()
        zhsend[x_rows_of(q)] = x_total(1 - zh, x_rows_of(q)).astype(BF16)
        begin(zh_copy(q))

    def write(rows, total):
        out_w[rows] = total
        one = pltpu.make_async_copy(out_w.at[rows], w_hbm.at[rows], load_sem.at[len(written)])
        one.start()
        written.append(one)

    def x_final(q):
        rows = x_rows_of(q)
        total = x_total(zh, rows)
        zh_copy(q).wait_recv()
        write(rows, total + zhrecv[rows].astype(F32))

    z_rows = pl.ds(X_ROWS, Z_ROWS)
    z_half = [pl.ds(X_ROWS, Z_ROWS // 2), pl.ds(X_ROWS + Z_ROWS // 2, Z_ROWS // 2)]

    def zw_copy(n):
        src = t_ref(x_order[n], 1 - zh, z_rows)
        return copy(src, zwrecv.at[n], other_run, sem_of(("zw", n)))

    def z_add(n):
        zw_copy(n).wait_recv()
        ref = t_ref(x_order[n], zh, z_rows)
        ref[...] = add(ref, zwrecv[n]).astype(BF16)

    def h_copy(step, plus):
        xx, half = {
            (1, True): (x2, 0), (1, False): (x2, 1), (2, True): (x1, 1),
            (2, False): (x3, 0), (3, True): (x1, 0), (3, False): (x3, 1),
        }[step, plus]
        slot = 2 * (step - 1) + (0 if plus else 1)
        src = t_ref(xx, zh, z_half[half])
        return copy(src, hrecv.at[slot], right if plus else left, sem_of(("h", step, plus)))

    def h_turn(plus):
        h_copy(1, plus).wait_recv()
        ref = t_ref(x1, zh, z_half[0]) if plus else t_ref(x3, zh, z_half[1])
        ref[...] = add(ref, hrecv[0 if plus else 1]).astype(BF16)
        begin(h_copy(3, plus))

    def h_final():
        for step in (2, 3):
            for plus in (True, False):
                h_copy(step, plus).wait_recv()
        low = add(t_ref(x, zh, z_half[0]), hrecv[4], hrecv[3])
        high = add(t_ref(x, zh, z_half[1]), hrecv[2], hrecv[5])
        write(z_rows, jnp.concatenate([low, high], axis=0))

    for code in AFTER:
        kind, p, q, r = code // 1000, code // 100 % 10, code // 10 % 10, code % 10
        if kind == 10:
            weight_grad(block_of(x_order[p], q, 1 - c))
            begin(core_copy(p, q))
        elif kind == 11:
            row_grad(p)
        elif kind == 12:
            weight_grad(block_of(x_order[p], q, c))
        elif kind == 13:
            core_sum(p, q)
        elif kind in (14, 15):
            begin(t_copy(kind - 13, p, q == 1))
        elif kind == 16:
            x_turn(p, q == 1)
        elif kind == 17:
            x_end(p)
        elif kind == 18:
            x_final(p)
        elif kind == 19:
            r_step(p, q, r == 1)
        elif kind == 20:
            r_end(p)
        elif kind == 21:
            r_final(p)
        elif kind == 22:
            begin(zw_copy(p))
        elif kind == 23:
            z_add(p)
        elif kind in (24, 25):
            begin(h_copy(kind - 23, p == 1))
        elif kind == 26:
            h_turn(p == 1)
        else:
            h_final()

    one = pltpu.make_async_copy(out_rows, rows_hbm, load_sem.at[len(written)])
    one.start()
    written.append(one)
    for one in written:
        one.wait()
    for one in sent:
        one.wait_send()
    for key in y_keys:
        y_copy(*key).wait_send()
    for p, d, k in z_keys:
        z_both(lambda one: one.wait_send(), p, d, order[k])
    for key in x_keys:
        x_copy(*key).wait_send()
    for key in core_keys:
        to_core(*key).wait_send()
    to_run().wait_send()


def finish(routes, probs, rows_hbm, grads_hbm, out_tok, out_gu, out_dn, rows, grads, buf, sem):
    copies = [
        pltpu.make_async_copy(grads.at[pl.ds(0, UNITS)], out_gu.at[0], sem.at[0]),
        pltpu.make_async_copy(grads.at[pl.ds(UNITS, UNITS)], out_gu.at[1], sem.at[1]),
        pltpu.make_async_copy(grads.at[pl.ds(2 * UNITS, UNITS)], out_dn, sem.at[2]),
    ]
    loads = [
        pltpu.make_async_copy(rows_hbm, rows, sem.at[5]),
        pltpu.make_async_copy(grads_hbm, grads, sem.at[6]),
    ]
    for load in loads:
        load.start()
    n_tok = out_tok.shape[0]
    picker, _ = slots(routes, probs)
    placed = jnp.concatenate([picker, jnp.zeros((n_tok - 2 * CAP, n_tok), F32)], axis=0).T
    placed = placed[:, : 2 * CAP]
    lane = lax.broadcasted_iota(jnp.int32, (n_tok, 2 * CAP), 1)
    low = jnp.where(lane < CAP, placed, 0.0).astype(BF16)
    high = jnp.where(lane >= CAP, placed, 0.0).astype(BF16)
    loads[1].wait()
    for one in copies:
        one.start()
    loads[0].wait()
    for n, part in enumerate((low, high)):
        at = pl.ds(n * (D // 2), D // 2)
        buf[:, at] = jnp.dot(part, rows[...], preferred_element_type=F32).astype(BF16)
        one = pltpu.make_async_copy(buf.at[:, at], out_tok.at[:, at], sem.at[3 + n])
        one.start()
        copies.append(one)
    for one in copies:
        one.wait()


def on_device(tokens_in, out_grad, routes, router_probs, gate_up, down_proj):
    vmem = pl.BlockSpec(memory_space=pltpu.VMEM)
    hbm = pl.BlockSpec(memory_space=pltpu.HBM)
    n_tok = tokens_in.shape[0]
    blocks = NY * NZ
    n_sems = 320
    routes, router_probs = routes.T, router_probs.T
    rows, grads = pl.pallas_call(
        kernel,
        out_shape=(
            jax.ShapeDtypeStruct((2 * CAP, D // 2), BF16),
            jax.ShapeDtypeStruct((3 * UNITS, COLS), F32),
        ),
        in_specs=[hbm] * 6,
        out_specs=(hbm, hbm),
        scratch_shapes=[
            pltpu.VMEM(routes.shape, routes.dtype),
            pltpu.VMEM(router_probs.shape, F32),
            pltpu.VMEM((2 * CAP, D // 2), BF16),
            pltpu.VMEM((3 * UNITS, COLS), F32),
            pltpu.VMEM((n_tok, D), BF16),
            pltpu.VMEM((n_tok, D), BF16),
            pltpu.VMEM((blocks, 2 * CAP, D), BF16),
            pltpu.VMEM((3 * UNITS, D), BF16),
            pltpu.VMEM((3 * UNITS, 2 * CAP * blocks), BF16),
            pltpu.VMEM((CAP * blocks, 2 * UNITS), BF16),
            pltpu.VMEM((NY, NZ, 2 * CAP, D // 2), BF16),
            pltpu.VMEM((7 * PARTS, NZ, 2 * CAP, PART), BF16),
            pltpu.VMEM((PARTS, NZ, 2 * CAP, PART), BF16),
            pltpu.VMEM((16, 3 * UNITS, COLS), BF16),
            pltpu.VMEM((8, 3 * UNITS, COLS), BF16),
            pltpu.VMEM((6, X_ROWS, COLS), BF16),
            pltpu.VMEM((X_ROWS, COLS), BF16),
            pltpu.VMEM((X_ROWS, COLS), BF16),
            pltpu.VMEM((4, Z_ROWS, COLS), BF16),
            pltpu.VMEM((6, Z_ROWS // 2, COLS), BF16),
            pltpu.SemaphoreType.DMA((7,)),
            pltpu.SemaphoreType.DMA((n_sems,)),
            pltpu.SemaphoreType.DMA((n_sems,)),
        ],
        compiler_params=pltpu.CompilerParams(
            collective_id=0, has_side_effects=True, vmem_limit_bytes=56 * 2**20
        ),
        cost_estimate=pl.CostEstimate(
            flops=6 * 10**9, bytes_accessed=4 * 2**20, transcendentals=2**15
        ),
        name="expert_backward",
    )(tokens_in, out_grad, routes, router_probs, gate_up, down_proj)
    return pl.pallas_call(
        finish,
        out_shape=(
            jax.ShapeDtypeStruct(tokens_in.shape, BF16),
            jax.ShapeDtypeStruct(gate_up.shape, F32),
            jax.ShapeDtypeStruct(down_proj.shape, F32),
        ),
        in_specs=[vmem, vmem, hbm, hbm],
        out_specs=(hbm, hbm, hbm),
        scratch_shapes=[
            pltpu.VMEM((2 * CAP, D // 2), BF16),
            pltpu.VMEM((3 * UNITS, COLS), F32),
            pltpu.VMEM((n_tok, D), BF16),
            pltpu.SemaphoreType.DMA((7,)),
        ],
        name="finish",
    )(routes, router_probs, rows, grads)


def solution(mesh):
    in_specs = (
        P(("dp", "expert"), None),
        P(("dp", "expert"), None),
        P(("dp", "expert"), None),
        P(("dp", "expert"), None),
        P(None, "expert", "dp"),
        P("expert", "dp"),
    )
    out_specs = (P(("dp", "expert"), None), P(None, "expert", "dp"), P("expert", "dp"))
    return jax.shard_map(
        on_device, mesh=mesh, in_specs=in_specs, out_specs=out_specs, check_vma=False
    )
```

```python
import jax
import jax.numpy as jnp
from jax import lax
from jax.experimental import pallas as pl
from jax.experimental.pallas import tpu as pltpu
from jax.sharding import PartitionSpec as P

MESH = pl.DeviceIdType.MESH
F32, BF16 = jnp.float32, jnp.bfloat16
NX, NY, NZ = 4, 8, 4
D = 4096
CAP = 8
COLS = 256
UNITS = 128
HALF = 3 * UNITS // 2
FIRST = 1408
PARTS = 4
PART = D // 2 // PARTS
CHUNKS = 2
X_ROWS = 256
CH = X_ROWS // CHUNKS
Z_ROWS = 3 * UNITS - X_ROWS

AFTER = (
    10010, 11000, 10000, 12100, 11100, 10100, 12010, 10110, 11200, 12310, 12300, 12110, 12000, 10210,
    10200, 13010, 14100, 13000, 22000, 14010, 11300, 14110, 14000, 12210, 13110, 10310, 13100, 22100,
    19010, 10300, 19011, 12200, 13200, 13210, 15010, 22200, 15100, 19110, 19111, 19211, 15110, 19210,
    16000, 16010, 15000, 19310, 19021, 19311, 16100, 13310, 19020, 16110, 13300, 22300, 23000, 19120,
    19221, 19121, 24000, 24100, 19220, 17000, 19320, 17100, 23100, 19031, 19130, 26100, 19321, 23200,
    25100, 26000, 19231, 19330, 20000, 25000, 20100, 20200, 23300, 20300, 21100, 18100, 18000, 27000,
    21000, 21200, 21300,
)
AT_ENDS = (
    11010, 21000, 11011, 20000, 12010, 10011, 10010, 12011, 40000, 30000, 11111, 11110, 11021, 11020,
    22100, 10111, 10110, 12021, 12020, 10021, 10020, 22000, 21010, 11121, 11120, 20010, 50000, 11031,
    11030, 10121, 50100, 22600, 22200, 10120, 12031, 12030, 10031, 22700, 10030, 11130, 21020, 11211,
    11210, 22110, 11041, 20020, 10211, 11131, 10210, 60000, 22010, 41000, 10130, 22500, 12041, 10041,
    11140, 10131, 22300, 11220, 10220, 11221, 10140, 22710, 11311, 22210, 11310, 22400, 11230, 10311,
    20030, 10221, 21030, 10310, 22020, 22120, 22720, 22610, 22220, 11231, 11321, 10230, 10321, 51100,
    11320, 11240, 51000, 10231, 10240, 10320, 11331, 22310, 22030, 22620, 10331, 61000, 11330, 11341,
    22530, 22510, 22130, 10341, 10330, 22430, 22630, 22320, 22420, 22730, 22230, 22330, 22410, 22520,
)
INSIDE = (
    21000, 11011, 11010, 20000, 12011, 12010, 10011, 10010, 40000, 11210, 11021, 30000, 21020, 21010,
    11211, 11111, 20010, 20020, 11110, 10021, 11020, 10211, 10111, 10110, 10210, 22100, 22000, 22700,
    11220, 12020, 50100, 50000, 12021, 11221, 11120, 11031, 11121, 11030, 12031, 22200, 21030, 10020,
    10221, 10120, 11311, 22600, 11310, 10220, 10311, 22020, 10031, 10121, 60000, 10310, 11231, 11130,
    22110, 20030, 22710, 11131, 22610, 22220, 12030, 22720, 22010, 11041, 22120, 10030, 22310, 11230,
    22620, 11320, 10231, 22210, 11321, 22510, 41000, 12041, 22500, 10131, 22130, 10041, 22300, 10230,
    10320, 22030, 22730, 11140, 10321, 22410, 22530, 10130, 22320, 51000, 22230, 11330, 10330, 11240,
    51100, 11331, 22520, 22330, 10140, 22400, 10331, 22630, 10240, 11341, 22430, 61000, 10341, 22420,
)


def slots(routes, probs):
    n_tok = routes.shape[1]
    chosen = routes[...] == 0
    weight = jnp.sum(jnp.where(chosen, probs[...], 0.0), axis=0, keepdims=True)
    member = jnp.sum(jnp.where(chosen, 1.0, 0.0), axis=0, keepdims=True)
    weight = jnp.broadcast_to(weight, (2 * CAP, n_tok))
    member = jnp.broadcast_to(member, (2 * CAP, n_tok))
    before = lax.broadcasted_iota(jnp.int32, (n_tok, n_tok), 0)
    upto = lax.broadcasted_iota(jnp.int32, (n_tok, n_tok), 1)
    prefix = jnp.where(before <= upto, 1.0, 0.0).astype(BF16)
    position = jnp.dot(member.astype(BF16), prefix, preferred_element_type=F32)
    slot = (lax.broadcasted_iota(jnp.int32, (2 * CAP, n_tok), 0) % CAP).astype(F32)
    picker = jnp.where((position - 1.0 == slot) & (member > 0.5), 1.0, 0.0)
    return picker, jnp.sum(picker * weight, axis=1, keepdims=True)


N_SEND, N_RECV = 14, 158


class Sems:
    def __init__(self):
        self.named, self.used = {}, 0

    def __call__(self, name, n=1):
        if name not in self.named:
            self.named[name] = self.used
            self.used += n
        return self.named[name]


def kernel(
    tok_hbm, og_hbm, routes_hbm, probs_hbm, gu_hbm, dn_hbm,
    rows_hbm, w_hbm,
    routes, probs, out_rows, out_w, tok, og, G, W, A_t, dH, R, yrecv, zrecv, T, crecv, xrecv, zhrecv, zhsend, zwrecv, hrecv,
    load_sem, send_sem, recv_sem,
):
    dp, ex = lax.axis_index("dp"), lax.axis_index("expert")
    x, zh, c = dp // 4, (dp // 2) % 2, dp % 2
    zl, y = ex // NY, ex % NY

    def at(x=x, zh=zh, c=c, zl=zl, y=y):
        return ((x * 2 + zh) * 2 + c, zl * NY + y)

    right, left = at(x=(x + 1) % NX), at(x=(x + NX - 1) % NX)
    north, south = at(y=(y + 1) % NY), at(y=(y + NY - 1) % NY)
    other_core, other_run = at(c=1 - c), at(zh=1 - zh)
    in_run = [at(zl=(zl + j) % NZ) for j in range(1, NZ)]

    barrier = pltpu.get_barrier_semaphore()
    peers = [right, left, north, south, other_core, other_run] + in_run
    for peer in peers:
        pl.semaphore_signal(barrier, inc=1, device_id=peer, device_id_type=MESH)

    def cols(i):
        return pl.ds(pl.multiple_of(i * COLS, COLS), COLS)

    mine = cols(dp)
    routing = [
        pltpu.make_async_copy(routes_hbm, routes, load_sem.at[5]),
        pltpu.make_async_copy(probs_hbm, probs, load_sem.at[6]),
    ]
    loads = [
        pltpu.make_async_copy(tok_hbm, tok, load_sem.at[0]),
        pltpu.make_async_copy(og_hbm, og, load_sem.at[1]),
        pltpu.make_async_copy(gu_hbm.at[0], W.at[pl.ds(0, UNITS), mine], load_sem.at[2]),
        pltpu.make_async_copy(gu_hbm.at[1], W.at[pl.ds(UNITS, UNITS), mine], load_sem.at[3]),
        pltpu.make_async_copy(dn_hbm, W.at[pl.ds(2 * UNITS, UNITS), mine], load_sem.at[4]),
    ]
    for load in routing + loads:
        load.start()
    for load in routing:
        load.wait()

    picker, slot_weight = slots(routes, probs)
    picker_b = picker.astype(BF16)
    own_block = y * NZ + zl
    for load in loads:
        load.wait()
    x_rows = jnp.dot(picker_b, tok[...], preferred_element_type=F32)
    g_rows = jnp.dot(picker_b, og[...], preferred_element_type=F32)
    e_rows = slot_weight * g_rows
    G[own_block] = jnp.concatenate([x_rows[:CAP], e_rows[CAP:]], axis=0).astype(BF16)

    pl.semaphore_wait(barrier, len(peers))

    sent, due = Sems(), Sems()

    def copy(src, dst, device, group, k):
        return pltpu.make_async_remote_copy(
            src_ref=src,
            dst_ref=dst,
            send_sem=send_sem.at[sent(group)],
            recv_sem=recv_sem.at[k],
            device_id=device,
            device_id_type=MESH,
        )

    def all_sent(group, ref):
        copy(ref, ref, other_core, group, 0).wait_send()

    def all_due(k, ref):
        copy(ref, ref, other_core, "rows", k).wait_recv()

    upper = zl // 2
    m = zl * (1 - upper) + (3 - zl) * upper
    order = [b * (1 - upper) + (3 - b) * upper for b in (m, 1 - m, 2, 3)]

    col_parts = [pl.ds(0, FIRST), pl.ds(FIRST, FIRST), pl.ds(2 * FIRST, D - 2 * FIRST)]

    def z_copy(part, d, zs, up):
        ref = G.at[(y + d) % NY * NZ + zs, :, col_parts[part]]
        to = (zl + (1 if up else NZ - 1)) % NZ
        k = due(("z", part, d), NZ - 1) + (zs - to + 2 * NZ - 1) % NZ
        return copy(ref, ref, at(zl=to), ("z", part), k)

    def z_due(part, d, zs):
        ref = G.at[(y + d) % NY * NZ + zs, :, col_parts[part]]
        return copy(ref, ref, north, ("z", part), due(("z", part, d), NZ - 1) + (zs - zl + 2 * NZ - 1) % NZ)

    def z_both(act, part, d, zs):
        @pl.when((zs <= zl) & (zl < NZ - 1))
        def _():
            act(z_copy(part, d, zs, True))

        @pl.when((zs >= zl) & (zl > 0))
        def _():
            act(z_copy(part, d, zs, False))

    def start(one):
        one.start()

    def hops(k, plus):
        return 4 if (k in (0, 3)) == plus else 3

    def y_copy(part, k, h, plus):
        src_y = (y + (NY - h + 1 if plus else h - 1)) % NY
        ref = G.at[src_y * NZ + order[k], :, col_parts[part]]
        return copy(ref, ref, north if plus else south, ("y", part), due(("y", part, k, h, plus)))

    def block_of(xx, zz, cc):
        return (xx * 2 + zz) * 2 + cc

    def w_ref(xx, zz, rows=pl.ds(0, 3 * UNITS), cc=c):
        return W.at[rows, cols(block_of(xx, zz, cc))]

    lo, hi = pl.ds(0, HALF), pl.ds(HALF, HALF)
    x1, x2, x3 = (x + 1) % NX, (x + 2) % NX, (x + 3) % NX
    runs = (zh, 1 - zh)

    def to_core(n, xx):
        ref = w_ref(xx, runs[n])
        return copy(ref, ref, other_core, "weights", due("core"))

    def to_run():
        return copy(w_ref(x, zh), w_ref(x, zh), other_run, "weights", due("w_run"))

    def x_copy(n, hop, plus):
        if hop == 1:
            ref = w_ref(x, runs[n])
        else:
            ref = w_ref(x3, runs[n], lo) if plus else w_ref(x1, runs[n], hi)
        return copy(ref, ref, right if plus else left, "weights", due(("x", n, hop, plus)))

    y_keys = [(p, k, h, plus) for p in range(3) for k in range(4 if p < 2 else 1) for plus in (True, False) for h in range(1, hops(k, plus) + 1)]

    def exchange(codes):
        taken = set()

        def take(one, *key):
            if key not in taken:
                taken.add(key)
                one().wait_recv()

        def take_y(*key):
            take(lambda: y_copy(*key), "y", *key)

        def take_z(p, d, k):
            take(lambda: z_due(p, d, order[k]), "z", p, d, k)

        for code in codes:
            kind, p, q, r, w = (code // 10**e % 10 for e in (4, 3, 2, 1, 0))
            if kind == 1:
                if r > 1:
                    take_y(p, q, r - 1, w == 1)
                elif q > 0:
                    take_z(p, 0, q)
                y_copy(p, q, r, w == 1).start()
            elif kind == 2:
                if r > 0:
                    take_z(p, q, r)
                elif q > 0:
                    take_y(p, 0, min(q, NY - q), q >= 4)
                z_both(start, p, q, order[r])
            elif kind == 3:
                to_run().start()
            elif kind == 4:
                if p == 1:
                    to_run().wait_recv()
                x_copy(p, 1, True).start()
                x_copy(p, 1, False).start()
                to_core(p, x).start()
            elif kind == 5:
                x_copy(p, 1, q == 1).wait_recv()
                x_copy(p, 2, q == 1).start()
                to_core(p, x3 if q == 1 else x1).start()
            else:
                x_copy(p, 2, True).wait_recv()
                x_copy(p, 2, False).wait_recv()
                to_core(p, x2).start()
        for key in y_keys:
            take_y(*key)
        all_due(due("core"), W.at[:, pl.ds(0, 8 * COLS)])

    for key in y_keys:
        due(("y", *key))

    @pl.when((zl == 0) | (zl == NZ - 1))
    def _():
        exchange(AT_ENDS)

    @pl.when((zl > 0) & (zl < NZ - 1))
    def _():
        exchange(INSIDE)

    for half in range(2):
        g = G[pl.ds(half * 16, 16)].reshape(256, D)
        pre = lax.dot_general(g, W[...], (((1,), (1,)), ((), ())), preferred_element_type=F32)
        pre = pre.reshape(16, 2 * CAP, 3 * UNITS)
        gate_pre = pre[:, :CAP, :UNITS]
        up_pre = pre[:, :CAP, UNITS : 2 * UNITS]
        hidden_grad = pre[:, CAP:, 2 * UNITS :]
        sig = 1.0 / (1.0 + jnp.exp(-gate_pre))
        activated = gate_pre * sig
        hidden = activated * up_pre
        up_grad = hidden_grad * activated
        gate_grad = hidden_grad * up_pre * sig * (1.0 + gate_pre * (1.0 - sig))
        zero = jnp.zeros_like(hidden)
        a = jnp.concatenate(
            [
                jnp.concatenate([gate_grad, up_grad, zero], axis=2),
                jnp.concatenate([zero, zero, hidden], axis=2),
            ],
            axis=1,
        ).reshape(256, 3 * UNITS)
        A_t[:, pl.ds(half * 256, 256)] = a.T.astype(BF16)
        grads = jnp.concatenate([gate_grad, up_grad], axis=2).reshape(128, 2 * UNITS)
        dH[pl.ds(half * 128, 128)] = grads.astype(BF16)

    def weight_grad(i):
        g = G[:, :, cols(i)].reshape(512, COLS)
        T[i] = jnp.dot(A_t[...], g, preferred_element_type=F32).astype(BF16)

    written = []
    x_order = [x2, x1, x3, x]

    def begin(one):
        one.start()

    def add(ref, *terms):
        total = ref[...].astype(F32)
        for term in terms:
            total = total + term.astype(F32)
        return total

    def core_copy(n, zz):
        i = block_of(x_order[n], zz, 1 - c)
        return copy(T.at[i], crecv.at[2 * n + zz], other_core, "cores", due(("c", n, zz)))

    def core_sum(n, zz):
        core_copy(n, zz).wait_recv()
        ref = T.at[block_of(x_order[n], zz, c)]
        ref[...] = add(ref, crecv[2 * n + zz]).astype(BF16)

    def r_part(yy, p):
        return R.at[yy, :, :, pl.ds(p * PART, PART)]

    def r_hops(p, plus):
        return 4 if (p % 2 == 0) == plus else 3

    r_slot = {}
    for plus in (True, False):
        for p in range(PARTS):
            for s in range(1, r_hops(p, plus) + 1):
                r_slot[p, s, plus] = len(r_slot)

    def r_dest(p, s, plus):
        d = r_hops(p, plus) - s + 1
        return (y + (d if plus else NY - d)) % NY

    def r_copy(p, s, plus):
        src, dst = r_part(r_dest(p, s, plus), p), yrecv.at[r_slot[p, s, plus]]
        return copy(src, dst, north if plus else south, "row_sums", due(("r", p, s, plus)))

    def r_step(p, s, plus):
        r_copy(p, s, plus).wait_recv()
        ref = r_part(r_dest(p, s + 1, plus), p)
        ref[...] = add(ref, yrecv[r_slot[p, s, plus]]).astype(BF16)
        begin(r_copy(p, s + 1, plus))

    def row_grad(p):
        parts = []
        for base in (0, D // 2):
            w = W[pl.ds(0, 2 * UNITS), pl.ds(base + p * PART, PART)]
            part = jnp.dot(dH[...], w, preferred_element_type=F32)
            parts.append(part.reshape(NY * NZ, CAP, PART))
        both = jnp.concatenate(parts, axis=1).astype(BF16)
        R[:, :, :, pl.ds(p * PART, PART)] = both.reshape(NY, NZ, 2 * CAP, PART)
        for plus in (True, False):
            begin(r_copy(p, 1, plus))

    def run_copy(p, zs):
        src = R.at[y, zs, :, pl.ds(p * PART, PART)]
        return copy(src, zrecv.at[p, zl], at(zl=zs), "rows", due(("run", p)))

    def r_end(p):
        ways = (True, False)
        for plus in ways:
            r_copy(p, r_hops(p, plus), plus).wait_recv()
        ref = r_part(y, p)
        terms = [yrecv[r_slot[p, r_hops(p, plus), plus]] for plus in ways]
        ref[...] = add(ref, *terms).astype(BF16)
        for j in range(1, NZ):
            begin(run_copy(p, (zl + j) % NZ))

    def r_final(p):
        others = [(zl + j) % NZ for j in range(1, NZ)]
        all_due(due(("run", p)), zrecv.at[p, pl.ds(0, NZ - 1)])
        here = pl.ds(p * PART, PART)
        total = add(R.at[y, zl, :, here], *[zrecv[p, zs] for zs in others])
        out_rows[:, here] = total.astype(BF16)

    def t_ref(xx, zz, rows):
        return T.at[block_of(xx, zz, c), rows]

    def x_rows_of(q):
        return pl.ds(q * CH, CH)

    def t_copy(step, q, plus):
        xx, zz = {
            (1, True): (x2, 0), (1, False): (x2, 1), (2, True): (x1, 1),
            (2, False): (x3, 0), (3, True): (x1, 0), (3, False): (x3, 1),
        }[step, plus]
        slot = 2 * (step - 1) + (0 if plus else 1)
        src, dst = t_ref(xx, zz, x_rows_of(q)), xrecv.at[slot, x_rows_of(q)]
        k = due(("t", q, plus) if step == 1 else ("t", q))
        return copy(src, dst, right if plus else left, "round_x", k)

    def x_turn(q, plus):
        t_copy(1, q, plus).wait_recv()
        ref = t_ref(x1, 0, x_rows_of(q)) if plus else t_ref(x3, 1, x_rows_of(q))
        ref[...] = add(ref, xrecv[0 if plus else 1, x_rows_of(q)]).astype(BF16)
        begin(t_copy(3, q, plus))

    def x_total(zz, rows):
        return add(t_ref(x, zz, rows), xrecv[4 - 2 * zz, rows], xrecv[3 + 2 * zz, rows])

    def zh_copy(q):
        rows = x_rows_of(q)
        return copy(zhsend.at[rows], zhrecv.at[rows], other_run, "sums", due(("zh", q)))

    def x_end(q):
        all_due(due(("t", q)), xrecv.at[pl.ds(0, 4), x_rows_of(0)])
        zhsend[x_rows_of(q)] = x_total(1 - zh, x_rows_of(q)).astype(BF16)
        begin(zh_copy(q))

    def write(rows, total):
        out_w[rows] = total
        one = pltpu.make_async_copy(out_w.at[rows], w_hbm.at[rows], load_sem.at[len(written)])
        one.start()
        written.append(one)

    def x_final(q):
        rows = x_rows_of(q)
        total = x_total(zh, rows)
        zh_copy(q).wait_recv()
        write(rows, total + zhrecv[rows].astype(F32))

    z_rows = pl.ds(X_ROWS, Z_ROWS)
    z_half = [pl.ds(X_ROWS, Z_ROWS // 2), pl.ds(X_ROWS + Z_ROWS // 2, Z_ROWS // 2)]

    def zw_copy(n):
        src = t_ref(x_order[n], 1 - zh, z_rows)
        return copy(src, zwrecv.at[n], other_run, "to_run", due(("zw", n)))

    def z_add(n):
        zw_copy(n).wait_recv()
        ref = t_ref(x_order[n], zh, z_rows)
        ref[...] = add(ref, zwrecv[n]).astype(BF16)

    def h_copy(step, plus):
        xx, half = {
            (1, True): (x2, 0), (1, False): (x2, 1), (2, True): (x1, 1),
            (2, False): (x3, 0), (3, True): (x1, 0), (3, False): (x3, 1),
        }[step, plus]
        slot = 2 * (step - 1) + (0 if plus else 1)
        src = t_ref(xx, zh, z_half[half])
        k = due(("h", plus) if step == 1 else "h")
        return copy(src, hrecv.at[slot], right if plus else left, "halves", k)

    def h_turn(plus):
        h_copy(1, plus).wait_recv()
        ref = t_ref(x1, zh, z_half[0]) if plus else t_ref(x3, zh, z_half[1])
        ref[...] = add(ref, hrecv[0 if plus else 1]).astype(BF16)
        begin(h_copy(3, plus))

    def h_final():
        all_due(due("h"), hrecv.at[pl.ds(0, 4)])
        low = add(t_ref(x, zh, z_half[0]), hrecv[4], hrecv[3])
        high = add(t_ref(x, zh, z_half[1]), hrecv[2], hrecv[5])
        write(z_rows, jnp.concatenate([low, high], axis=0))

    for code in AFTER:
        kind, p, q, r = code // 1000, code // 100 % 10, code // 10 % 10, code % 10
        if kind == 10:
            weight_grad(block_of(x_order[p], q, 1 - c))
            begin(core_copy(p, q))
        elif kind == 11:
            row_grad(p)
        elif kind == 12:
            weight_grad(block_of(x_order[p], q, c))
        elif kind == 13:
            core_sum(p, q)
        elif kind in (14, 15):
            begin(t_copy(kind - 13, p, q == 1))
        elif kind == 16:
            x_turn(p, q == 1)
        elif kind == 17:
            x_end(p)
        elif kind == 18:
            x_final(p)
        elif kind == 19:
            r_step(p, q, r == 1)
        elif kind == 20:
            r_end(p)
        elif kind == 21:
            r_final(p)
        elif kind == 22:
            begin(zw_copy(p))
        elif kind == 23:
            z_add(p)
        elif kind in (24, 25):
            begin(h_copy(kind - 23, p == 1))
        elif kind == 26:
            h_turn(p == 1)
        else:
            h_final()

    one = pltpu.make_async_copy(out_rows, rows_hbm, load_sem.at[len(written)])
    one.start()
    written.append(one)
    for one in written:
        one.wait()
    for part in range(3):
        all_sent(("y", part), G.at[pl.ds(0, 28 if part < 2 else 7), :, col_parts[part]])

    @pl.when((zl == 0) | (zl == NZ - 1))
    def _():
        for part in range(3):
            all_sent(("z", part), G.at[pl.ds(0, 1 if part < 2 else NY), :, col_parts[part]])

    @pl.when((zl > 0) & (zl < NZ - 1))
    def _():
        for part in range(2):
            all_sent(("z", part), G.at[pl.ds(0, 5), :, col_parts[part]])
        all_sent(("z", 2), G.at[pl.ds(0, 20), :, pl.ds(0, 2 * (D - 2 * FIRST))])

    all_sent("weights", W.at[:, pl.ds(0, 15 * COLS)])
    all_sent("cores", T.at[pl.ds(0, 8)])
    all_sent("row_sums", yrecv)
    all_sent("rows", zrecv.at[pl.ds(0, PARTS * (NZ - 1) // NZ)])
    all_sent("round_x", xrecv)
    all_sent("sums", zhsend)
    all_sent("to_run", zwrecv)
    all_sent("halves", hrecv)
    if (sent.used, due.used) != (N_SEND, N_RECV):
        raise ValueError(f"{sent.used} {due.used}")


def finish(routes, probs, rows_hbm, grads_hbm, out_tok, out_gu, out_dn, rows, grads, buf, sem):
    copies = [
        pltpu.make_async_copy(grads.at[pl.ds(0, UNITS)], out_gu.at[0], sem.at[0]),
        pltpu.make_async_copy(grads.at[pl.ds(UNITS, UNITS)], out_gu.at[1], sem.at[1]),
        pltpu.make_async_copy(grads.at[pl.ds(2 * UNITS, UNITS)], out_dn, sem.at[2]),
    ]
    loads = [
        pltpu.make_async_copy(rows_hbm, rows, sem.at[5]),
        pltpu.make_async_copy(grads_hbm, grads, sem.at[6]),
    ]
    for load in loads:
        load.start()
    n_tok = out_tok.shape[0]
    picker, _ = slots(routes, probs)
    placed = jnp.concatenate([picker, jnp.zeros((n_tok - 2 * CAP, n_tok), F32)], axis=0).T
    placed = placed[:, : 2 * CAP]
    lane = lax.broadcasted_iota(jnp.int32, (n_tok, 2 * CAP), 1)
    low = jnp.where(lane < CAP, placed, 0.0).astype(BF16)
    high = jnp.where(lane >= CAP, placed, 0.0).astype(BF16)
    loads[1].wait()
    for one in copies:
        one.start()
    loads[0].wait()
    for n, part in enumerate((low, high)):
        at = pl.ds(n * (D // 2), D // 2)
        buf[:, at] = jnp.dot(part, rows[...], preferred_element_type=F32).astype(BF16)
        one = pltpu.make_async_copy(buf.at[:, at], out_tok.at[:, at], sem.at[3 + n])
        one.start()
        copies.append(one)
    for one in copies:
        one.wait()


def on_device(tokens_in, out_grad, routes, router_probs, gate_up, down_proj):
    vmem = pl.BlockSpec(memory_space=pltpu.VMEM)
    hbm = pl.BlockSpec(memory_space=pltpu.HBM)
    n_tok = tokens_in.shape[0]
    blocks = NY * NZ
    routes, router_probs = routes.T, router_probs.T
    rows, grads = pl.pallas_call(
        kernel,
        out_shape=(
            jax.ShapeDtypeStruct((2 * CAP, D // 2), BF16),
            jax.ShapeDtypeStruct((3 * UNITS, COLS), F32),
        ),
        in_specs=[hbm] * 6,
        out_specs=(hbm, hbm),
        scratch_shapes=[
            pltpu.VMEM(routes.shape, routes.dtype),
            pltpu.VMEM(router_probs.shape, F32),
            pltpu.VMEM((2 * CAP, D // 2), BF16),
            pltpu.VMEM((3 * UNITS, COLS), F32),
            pltpu.VMEM((n_tok, D), BF16),
            pltpu.VMEM((n_tok, D), BF16),
            pltpu.VMEM((blocks, 2 * CAP, D), BF16),
            pltpu.VMEM((3 * UNITS, D), BF16),
            pltpu.VMEM((3 * UNITS, 2 * CAP * blocks), BF16),
            pltpu.VMEM((CAP * blocks, 2 * UNITS), BF16),
            pltpu.VMEM((NY, NZ, 2 * CAP, D // 2), BF16),
            pltpu.VMEM((7 * PARTS, NZ, 2 * CAP, PART), BF16),
            pltpu.VMEM((PARTS, NZ, 2 * CAP, PART), BF16),
            pltpu.VMEM((16, 3 * UNITS, COLS), BF16),
            pltpu.VMEM((8, 3 * UNITS, COLS), BF16),
            pltpu.VMEM((6, X_ROWS, COLS), BF16),
            pltpu.VMEM((X_ROWS, COLS), BF16),
            pltpu.VMEM((X_ROWS, COLS), BF16),
            pltpu.VMEM((4, Z_ROWS, COLS), BF16),
            pltpu.VMEM((6, Z_ROWS // 2, COLS), BF16),
            pltpu.SemaphoreType.DMA((7,)),
            pltpu.SemaphoreType.DMA((N_SEND,)),
            pltpu.SemaphoreType.DMA((N_RECV,)),
        ],
        compiler_params=pltpu.CompilerParams(
            collective_id=0, has_side_effects=True, vmem_limit_bytes=56 * 2**20
        ),
        cost_estimate=pl.CostEstimate(
            flops=6 * 10**9, bytes_accessed=4 * 2**20, transcendentals=2**15
        ),
        name="expert_backward",
    )(tokens_in, out_grad, routes, router_probs, gate_up, down_proj)
    return pl.pallas_call(
        finish,
        out_shape=(
            jax.ShapeDtypeStruct(tokens_in.shape, BF16),
            jax.ShapeDtypeStruct(gate_up.shape, F32),
            jax.ShapeDtypeStruct(down_proj.shape, F32),
        ),
        in_specs=[vmem, vmem, hbm, hbm],
        out_specs=(hbm, hbm, hbm),
        scratch_shapes=[
            pltpu.VMEM((2 * CAP, D // 2), BF16),
            pltpu.VMEM((3 * UNITS, COLS), F32),
            pltpu.VMEM((n_tok, D), BF16),
            pltpu.SemaphoreType.DMA((7,)),
        ],
        name="finish",
    )(routes, router_probs, rows, grads)


def solution(mesh):
    in_specs = (
        P(("dp", "expert"), None),
        P(("dp", "expert"), None),
        P(("dp", "expert"), None),
        P(("dp", "expert"), None),
        P(None, "expert", "dp"),
        P("expert", "dp"),
    )
    out_specs = (P(("dp", "expert"), None), P(None, "expert", "dp"), P("expert", "dp"))
    return jax.shard_map(
        on_device, mesh=mesh, in_specs=in_specs, out_specs=out_specs, check_vma=False
    )
```

```python
import jax
import jax.numpy as jnp
from jax import lax
from jax.experimental import pallas as pl
from jax.experimental.pallas import tpu as pltpu
from jax.sharding import PartitionSpec as P

MESH = pl.DeviceIdType.MESH
F32, BF16 = jnp.float32, jnp.bfloat16
NX, NY, NZ = 4, 8, 4
D = 4096
CAP = 8
COLS = 256
UNITS = 128
HALF = 3 * UNITS // 2
FIRST = 1408
PARTS = 4
PART = D // 2 // PARTS
CHUNKS = 2
X_ROWS = 256
CH = X_ROWS // CHUNKS
Z_ROWS = 3 * UNITS - X_ROWS

AFTER = (
    10010, 11000, 10000, 12100, 11100, 10100, 12010, 10110, 11200, 12310, 12300, 12110, 12000, 10210,
    10200, 13010, 14100, 13000, 22000, 14010, 11300, 14110, 14000, 12210, 13110, 10310, 13100, 22100,
    19010, 10300, 19011, 12200, 13200, 13210, 15010, 22200, 15100, 19110, 19111, 19211, 15110, 19210,
    16000, 16010, 15000, 19310, 19021, 19311, 16100, 13310, 19020, 16110, 13300, 22300, 23000, 19120,
    19221, 19121, 24000, 24100, 19220, 17000, 19320, 17100, 23100, 19031, 19130, 26100, 19321, 23200,
    25100, 26000, 19231, 19330, 20000, 25000, 20100, 20200, 23300, 20300, 21100, 18100, 18000, 27000,
    21000, 21200, 21300,
)
AT_ENDS = (
    21000, 12010, 11010, 11011, 20000, 10010, 12011, 40000, 10011, 30000, 11110, 12020, 11111, 22100,
    11021, 10110, 11020, 10111, 10021, 22000, 12021, 50100, 10020, 20010, 11121, 11120, 11031, 22200,
    11030, 10121, 22600, 10120, 50000, 12031, 21010, 12030, 11130, 22700, 10031, 11210, 11211, 22110,
    10030, 11131, 21020, 10211, 10130, 10210, 22500, 22300, 10131, 60000, 12041, 11041, 11221, 11140,
    11220, 41000, 10140, 10220, 10041, 11311, 11310, 10311, 11230, 22010, 22120, 10221, 22400, 20020,
    22220, 11231, 22020, 22720, 21030, 10310, 11321, 22610, 10230, 20030, 22210, 10321, 11320, 51100,
    22620, 51000, 11240, 10320, 11331, 22510, 22710, 10331, 22310, 22730, 11330, 22230, 10240, 10231,
    22530, 11341, 61000, 22030, 10330, 10341, 22130, 22520, 22410, 22420, 22330, 22320, 22430, 22630,
)
INSIDE = (
    21000, 11011, 11010, 12010, 40000, 20000, 12011, 10011, 10010, 11021, 11111, 11210, 30000, 11020,
    21010, 21020, 11211, 20010, 20020, 10021, 10111, 10210, 22100, 11110, 50000, 10211, 22000, 12020,
    22700, 12021, 11120, 11031, 11221, 10110, 10020, 11220, 11121, 22200, 22600, 11030, 50100, 10121,
    21030, 11310, 12031, 11311, 10311, 10310, 10221, 22020, 12030, 20030, 10120, 22120, 22110, 11231,
    10031, 22710, 22220, 11131, 11130, 22010, 60000, 22720, 22210, 11320, 22310, 10220, 11041, 10231,
    11230, 22620, 11321, 22510, 22130, 22730, 22500, 41000, 12041, 10030, 10320, 22300, 10131, 10230,
    22610, 22230, 22030, 22530, 10041, 10321, 10130, 22320, 11331, 10330, 22410, 51100, 51000, 22400,
    22330, 10240, 11140, 10331, 22520, 11240, 11330, 11341, 22430, 10140, 22420, 61000, 22630, 10341,
)


def slots(routes, probs):
    n_tok = routes.shape[1]
    chosen = routes[...] == 0
    weight = jnp.sum(jnp.where(chosen, probs[...], 0.0), axis=0, keepdims=True)
    member = jnp.sum(jnp.where(chosen, 1.0, 0.0), axis=0, keepdims=True)
    weight = jnp.broadcast_to(weight, (2 * CAP, n_tok))
    member = jnp.broadcast_to(member, (2 * CAP, n_tok))
    before = lax.broadcasted_iota(jnp.int32, (n_tok, n_tok), 0)
    upto = lax.broadcasted_iota(jnp.int32, (n_tok, n_tok), 1)
    prefix = jnp.where(before <= upto, 1.0, 0.0).astype(BF16)
    position = jnp.dot(member.astype(BF16), prefix, preferred_element_type=F32)
    slot = (lax.broadcasted_iota(jnp.int32, (2 * CAP, n_tok), 0) % CAP).astype(F32)
    picker = jnp.where((position - 1.0 == slot) & (member > 0.5), 1.0, 0.0)
    return picker, jnp.sum(picker * weight, axis=1, keepdims=True)


N_SEND, N_RECV = 14, 158


class Sems:
    def __init__(self):
        self.named, self.used = {}, 0

    def __call__(self, name, n=1):
        if name not in self.named:
            self.named[name] = self.used
            self.used += n
        return self.named[name]


def kernel(
    tok_hbm, og_hbm, routes_hbm, probs_hbm, gu_hbm, dn_hbm,
    rows_hbm, w_hbm,
    routes, probs, out_rows, out_w, tok, og, G, W, A_t, dH, R, yrecv, zrecv, T, crecv, xrecv, zhrecv, zhsend, zwrecv, hrecv,
    load_sem, send_sem, recv_sem,
):
    dp, ex = lax.axis_index("dp"), lax.axis_index("expert")
    x, zh, c = dp // 4, (dp // 2) % 2, dp % 2
    zl, y = ex // NY, ex % NY

    def at(x=x, zh=zh, c=c, zl=zl, y=y):
        return ((x * 2 + zh) * 2 + c, zl * NY + y)

    right, left = at(x=(x + 1) % NX), at(x=(x + NX - 1) % NX)
    north, south = at(y=(y + 1) % NY), at(y=(y + NY - 1) % NY)
    other_core, other_run = at(c=1 - c), at(zh=1 - zh)
    in_run = [at(zl=(zl + j) % NZ) for j in range(1, NZ)]

    barrier = pltpu.get_barrier_semaphore()
    peers = [right, left, north, south, other_core, other_run] + in_run
    for peer in peers:
        pl.semaphore_signal(barrier, inc=1, device_id=peer, device_id_type=MESH)

    def cols(i):
        return pl.ds(pl.multiple_of(i * COLS, COLS), COLS)

    mine = cols(dp)
    routing = [
        pltpu.make_async_copy(routes_hbm, routes, load_sem.at[5]),
        pltpu.make_async_copy(probs_hbm, probs, load_sem.at[6]),
    ]
    loads = [
        pltpu.make_async_copy(tok_hbm, tok, load_sem.at[0]),
        pltpu.make_async_copy(og_hbm, og, load_sem.at[1]),
        pltpu.make_async_copy(gu_hbm.at[0], W.at[pl.ds(0, UNITS), mine], load_sem.at[2]),
        pltpu.make_async_copy(gu_hbm.at[1], W.at[pl.ds(UNITS, UNITS), mine], load_sem.at[3]),
        pltpu.make_async_copy(dn_hbm, W.at[pl.ds(2 * UNITS, UNITS), mine], load_sem.at[4]),
    ]
    for load in routing + loads:
        load.start()
    for load in routing:
        load.wait()

    picker, slot_weight = slots(routes, probs)
    picker_b = picker.astype(BF16)
    own_block = y * NZ + zl
    for load in loads:
        load.wait()
    x_rows = jnp.dot(picker_b, tok[...], preferred_element_type=F32)
    g_rows = jnp.dot(picker_b, og[...], preferred_element_type=F32)
    e_rows = slot_weight * g_rows
    G[own_block] = jnp.concatenate([x_rows[:CAP], e_rows[CAP:]], axis=0).astype(BF16)

    pl.semaphore_wait(barrier, len(peers))

    sent, due = Sems(), Sems()

    def copy(src, dst, device, group, k):
        return pltpu.make_async_remote_copy(
            src_ref=src,
            dst_ref=dst,
            send_sem=send_sem.at[sent(group)],
            recv_sem=recv_sem.at[k],
            device_id=device,
            device_id_type=MESH,
        )

    def all_sent(group, ref):
        copy(ref, ref, other_core, group, 0).wait_send()

    def all_due(k, ref):
        copy(ref, ref, other_core, "rows", k).wait_recv()

    upper = zl // 2
    m = zl * (1 - upper) + (3 - zl) * upper
    order = [b * (1 - upper) + (3 - b) * upper for b in (m, 1 - m, 2, 3)]

    col_parts = [pl.ds(0, FIRST), pl.ds(FIRST, FIRST), pl.ds(2 * FIRST, D - 2 * FIRST)]

    def z_copy(part, d, zs, up):
        ref = G.at[(y + d) % NY * NZ + zs, :, col_parts[part]]
        to = (zl + (1 if up else NZ - 1)) % NZ
        k = due(("z", part, d), NZ - 1) + (zs - to + 2 * NZ - 1) % NZ
        return copy(ref, ref, at(zl=to), ("z", part), k)

    def z_due(part, d, zs):
        ref = G.at[(y + d) % NY * NZ + zs, :, col_parts[part]]
        return copy(ref, ref, north, ("z", part), due(("z", part, d), NZ - 1) + (zs - zl + 2 * NZ - 1) % NZ)

    def z_both(act, part, d, zs):
        @pl.when((zs <= zl) & (zl < NZ - 1))
        def _():
            act(z_copy(part, d, zs, True))

        @pl.when((zs >= zl) & (zl > 0))
        def _():
            act(z_copy(part, d, zs, False))

    def start(one):
        one.start()

    def hops(k, plus):
        return 4 if (k in (0, 3)) == plus else 3

    def y_copy(part, k, h, plus):
        src_y = (y + (NY - h + 1 if plus else h - 1)) % NY
        ref = G.at[src_y * NZ + order[k], :, col_parts[part]]
        return copy(ref, ref, north if plus else south, ("y", part), due(("y", part, k, h, plus)))

    def block_of(xx, zz, cc):
        return (xx * 2 + zz) * 2 + cc

    def w_ref(xx, zz, rows=pl.ds(0, 3 * UNITS), cc=c):
        return W.at[rows, cols(block_of(xx, zz, cc))]

    lo, hi = pl.ds(0, HALF), pl.ds(HALF, HALF)
    x1, x2, x3 = (x + 1) % NX, (x + 2) % NX, (x + 3) % NX
    runs = (zh, 1 - zh)

    def to_core(n, xx):
        ref = w_ref(xx, runs[n])
        return copy(ref, ref, other_core, "weights", due("core"))

    def to_run():
        return copy(w_ref(x, zh), w_ref(x, zh), other_run, "weights", due("w_run"))

    def x_copy(n, hop, plus):
        if hop == 1:
            ref = w_ref(x, runs[n])
        else:
            ref = w_ref(x3, runs[n], lo) if plus else w_ref(x1, runs[n], hi)
        return copy(ref, ref, right if plus else left, "weights", due(("x", n, hop, plus)))

    y_keys = [(p, k, h, plus) for p in range(3) for k in range(4 if p < 2 else 1) for plus in (True, False) for h in range(1, hops(k, plus) + 1)]

    def exchange(codes):
        taken = set()

        def take(one, *key):
            if key not in taken:
                taken.add(key)
                one().wait_recv()

        def take_y(*key):
            take(lambda: y_copy(*key), "y", *key)

        def take_z(p, d, k):
            take(lambda: z_due(p, d, order[k]), "z", p, d, k)

        for code in codes:
            kind, p, q, r, w = (code // 10**e % 10 for e in (4, 3, 2, 1, 0))
            if kind == 1:
                if r > 1:
                    take_y(p, q, r - 1, w == 1)
                elif q > 0:
                    take_z(p, 0, q)
                y_copy(p, q, r, w == 1).start()
            elif kind == 2:
                if r > 0:
                    take_z(p, q, r)
                elif q > 0:
                    take_y(p, 0, min(q, NY - q), q >= 4)
                z_both(start, p, q, order[r])
            elif kind == 3:
                to_run().start()
            elif kind == 4:
                if p == 1:
                    to_run().wait_recv()
                x_copy(p, 1, True).start()
                x_copy(p, 1, False).start()
                to_core(p, x).start()
            elif kind == 5:
                x_copy(p, 1, q == 1).wait_recv()
                x_copy(p, 2, q == 1).start()
                to_core(p, x3 if q == 1 else x1).start()
            else:
                x_copy(p, 2, True).wait_recv()
                x_copy(p, 2, False).wait_recv()
                to_core(p, x2).start()
        for key in y_keys:
            take_y(*key)
        all_due(due("core"), W.at[:, pl.ds(0, 8 * COLS)])

    for key in y_keys:
        due(("y", *key))

    @pl.when((zl == 0) | (zl == NZ - 1))
    def _():
        exchange(AT_ENDS)

    @pl.when((zl > 0) & (zl < NZ - 1))
    def _():
        exchange(INSIDE)

    for half in range(2):
        g = G[pl.ds(half * 16, 16)].reshape(256, D)
        pre = lax.dot_general(g, W[...], (((1,), (1,)), ((), ())), preferred_element_type=F32)
        pre = pre.reshape(16, 2 * CAP, 3 * UNITS)
        gate_pre = pre[:, :CAP, :UNITS]
        up_pre = pre[:, :CAP, UNITS : 2 * UNITS]
        hidden_grad = pre[:, CAP:, 2 * UNITS :]
        sig = 1.0 / (1.0 + jnp.exp(-gate_pre))
        activated = gate_pre * sig
        hidden = activated * up_pre
        up_grad = hidden_grad * activated
        gate_grad = hidden_grad * up_pre * sig * (1.0 + gate_pre * (1.0 - sig))
        zero = jnp.zeros_like(hidden)
        a = jnp.concatenate(
            [
                jnp.concatenate([gate_grad, up_grad, zero], axis=2),
                jnp.concatenate([zero, zero, hidden], axis=2),
            ],
            axis=1,
        ).reshape(256, 3 * UNITS)
        A_t[:, pl.ds(half * 256, 256)] = a.T.astype(BF16)
        grads = jnp.concatenate([gate_grad, up_grad], axis=2).reshape(128, 2 * UNITS)
        dH[pl.ds(half * 128, 128)] = grads.astype(BF16)

    def weight_grad(i):
        g = G[:, :, cols(i)].reshape(512, COLS)
        T[i] = jnp.dot(A_t[...], g, preferred_element_type=F32).astype(BF16)

    written = []
    x_order = [x2, x1, x3, x]

    def begin(one):
        one.start()

    def add(ref, *terms):
        total = ref[...].astype(F32)
        for term in terms:
            total = total + term.astype(F32)
        return total

    def core_copy(n, zz):
        i = block_of(x_order[n], zz, 1 - c)
        return copy(T.at[i], crecv.at[2 * n + zz], other_core, "cores", due(("c", n, zz)))

    def core_sum(n, zz):
        core_copy(n, zz).wait_recv()
        ref = T.at[block_of(x_order[n], zz, c)]
        ref[...] = add(ref, crecv[2 * n + zz]).astype(BF16)

    def r_part(yy, p):
        return R.at[yy, :, :, pl.ds(p * PART, PART)]

    def r_hops(p, plus):
        return 4 if (p % 2 == 0) == plus else 3

    r_slot = {}
    for plus in (True, False):
        for p in range(PARTS):
            for s in range(1, r_hops(p, plus) + 1):
                r_slot[p, s, plus] = len(r_slot)

    def r_dest(p, s, plus):
        d = r_hops(p, plus) - s + 1
        return (y + (d if plus else NY - d)) % NY

    def r_copy(p, s, plus):
        src, dst = r_part(r_dest(p, s, plus), p), yrecv.at[r_slot[p, s, plus]]
        return copy(src, dst, north if plus else south, "row_sums", due(("r", p, s, plus)))

    def r_step(p, s, plus):
        r_copy(p, s, plus).wait_recv()
        ref = r_part(r_dest(p, s + 1, plus), p)
        ref[...] = add(ref, yrecv[r_slot[p, s, plus]]).astype(BF16)
        begin(r_copy(p, s + 1, plus))

    def row_grad(p):
        parts = []
        for base in (0, D // 2):
            w = W[pl.ds(0, 2 * UNITS), pl.ds(base + p * PART, PART)]
            part = jnp.dot(dH[...], w, preferred_element_type=F32)
            parts.append(part.reshape(NY * NZ, CAP, PART))
        both = jnp.concatenate(parts, axis=1).astype(BF16)
        R[:, :, :, pl.ds(p * PART, PART)] = both.reshape(NY, NZ, 2 * CAP, PART)
        for plus in (True, False):
            begin(r_copy(p, 1, plus))

    def run_copy(p, zs):
        src = R.at[y, zs, :, pl.ds(p * PART, PART)]
        return copy(src, zrecv.at[p, zl], at(zl=zs), "rows", due(("run", p)))

    def r_end(p):
        ways = (True, False)
        for plus in ways:
            r_copy(p, r_hops(p, plus), plus).wait_recv()
        ref = r_part(y, p)
        terms = [yrecv[r_slot[p, r_hops(p, plus), plus]] for plus in ways]
        ref[...] = add(ref, *terms).astype(BF16)
        for j in range(1, NZ):
            begin(run_copy(p, (zl + j) % NZ))

    def r_final(p):
        others = [(zl + j) % NZ for j in range(1, NZ)]
        all_due(due(("run", p)), zrecv.at[p, pl.ds(0, NZ - 1)])
        here = pl.ds(p * PART, PART)
        total = add(R.at[y, zl, :, here], *[zrecv[p, zs] for zs in others])
        out_rows[:, here] = total.astype(BF16)

    def t_ref(xx, zz, rows):
        return T.at[block_of(xx, zz, c), rows]

    def x_rows_of(q):
        return pl.ds(q * CH, CH)

    def t_copy(step, q, plus):
        xx, zz = {
            (1, True): (x2, 0), (1, False): (x2, 1), (2, True): (x1, 1),
            (2, False): (x3, 0), (3, True): (x1, 0), (3, False): (x3, 1),
        }[step, plus]
        slot = 2 * (step - 1) + (0 if plus else 1)
        src, dst = t_ref(xx, zz, x_rows_of(q)), xrecv.at[slot, x_rows_of(q)]
        k = due(("t", q, plus) if step == 1 else ("t", q))
        return copy(src, dst, right if plus else left, "round_x", k)

    def x_turn(q, plus):
        t_copy(1, q, plus).wait_recv()
        ref = t_ref(x1, 0, x_rows_of(q)) if plus else t_ref(x3, 1, x_rows_of(q))
        ref[...] = add(ref, xrecv[0 if plus else 1, x_rows_of(q)]).astype(BF16)
        begin(t_copy(3, q, plus))

    def x_total(zz, rows):
        return add(t_ref(x, zz, rows), xrecv[4 - 2 * zz, rows], xrecv[3 + 2 * zz, rows])

    def zh_copy(q):
        rows = x_rows_of(q)
        return copy(zhsend.at[rows], zhrecv.at[rows], other_run, "sums", due(("zh", q)))

    def x_end(q):
        all_due(due(("t", q)), xrecv.at[pl.ds(0, 4), x_rows_of(0)])
        zhsend[x_rows_of(q)] = x_total(1 - zh, x_rows_of(q)).astype(BF16)
        begin(zh_copy(q))

    def write(rows, total):
        out_w[rows] = total
        one = pltpu.make_async_copy(out_w.at[rows], w_hbm.at[rows], load_sem.at[len(written)])
        one.start()
        written.append(one)

    def x_final(q):
        rows = x_rows_of(q)
        total = x_total(zh, rows)
        zh_copy(q).wait_recv()
        write(rows, total + zhrecv[rows].astype(F32))

    z_rows = pl.ds(X_ROWS, Z_ROWS)
    z_half = [pl.ds(X_ROWS, Z_ROWS // 2), pl.ds(X_ROWS + Z_ROWS // 2, Z_ROWS // 2)]

    def zw_copy(n):
        src = t_ref(x_order[n], 1 - zh, z_rows)
        return copy(src, zwrecv.at[n], other_run, "to_run", due(("zw", n)))

    def z_add(n):
        zw_copy(n).wait_recv()
        ref = t_ref(x_order[n], zh, z_rows)
        ref[...] = add(ref, zwrecv[n]).astype(BF16)

    def h_copy(step, plus):
        xx, half = {
            (1, True): (x2, 0), (1, False): (x2, 1), (2, True): (x1, 1),
            (2, False): (x3, 0), (3, True): (x1, 0), (3, False): (x3, 1),
        }[step, plus]
        slot = 2 * (step - 1) + (0 if plus else 1)
        src = t_ref(xx, zh, z_half[half])
        k = due(("h", plus) if step == 1 else "h")
        return copy(src, hrecv.at[slot], right if plus else left, "halves", k)

    def h_turn(plus):
        h_copy(1, plus).wait_recv()
        ref = t_ref(x1, zh, z_half[0]) if plus else t_ref(x3, zh, z_half[1])
        ref[...] = add(ref, hrecv[0 if plus else 1]).astype(BF16)
        begin(h_copy(3, plus))

    def h_final():
        all_due(due("h"), hrecv.at[pl.ds(0, 4)])
        low = add(t_ref(x, zh, z_half[0]), hrecv[4], hrecv[3])
        high = add(t_ref(x, zh, z_half[1]), hrecv[2], hrecv[5])
        write(z_rows, jnp.concatenate([low, high], axis=0))

    for code in AFTER:
        kind, p, q, r = code // 1000, code // 100 % 10, code // 10 % 10, code % 10
        if kind == 10:
            weight_grad(block_of(x_order[p], q, 1 - c))
            begin(core_copy(p, q))
        elif kind == 11:
            row_grad(p)
        elif kind == 12:
            weight_grad(block_of(x_order[p], q, c))
        elif kind == 13:
            core_sum(p, q)
        elif kind in (14, 15):
            begin(t_copy(kind - 13, p, q == 1))
        elif kind == 16:
            x_turn(p, q == 1)
        elif kind == 17:
            x_end(p)
        elif kind == 18:
            x_final(p)
        elif kind == 19:
            r_step(p, q, r == 1)
        elif kind == 20:
            r_end(p)
        elif kind == 21:
            r_final(p)
        elif kind == 22:
            begin(zw_copy(p))
        elif kind == 23:
            z_add(p)
        elif kind in (24, 25):
            begin(h_copy(kind - 23, p == 1))
        elif kind == 26:
            h_turn(p == 1)
        else:
            h_final()

    one = pltpu.make_async_copy(out_rows, rows_hbm, load_sem.at[len(written)])
    one.start()
    written.append(one)
    for one in written:
        one.wait()
    for part in range(3):
        all_sent(("y", part), G.at[pl.ds(0, 28 if part < 2 else 7), :, col_parts[part]])

    @pl.when((zl == 0) | (zl == NZ - 1))
    def _():
        for part in range(3):
            all_sent(("z", part), G.at[pl.ds(0, 1 if part < 2 else NY), :, col_parts[part]])

    @pl.when((zl > 0) & (zl < NZ - 1))
    def _():
        for part in range(2):
            all_sent(("z", part), G.at[pl.ds(0, 5), :, col_parts[part]])
        all_sent(("z", 2), G.at[pl.ds(0, 20), :, pl.ds(0, 2 * (D - 2 * FIRST))])

    all_sent("weights", W.at[:, pl.ds(0, 15 * COLS)])
    all_sent("cores", T.at[pl.ds(0, 8)])
    all_sent("row_sums", yrecv)
    all_sent("rows", zrecv.at[pl.ds(0, PARTS * (NZ - 1) // NZ)])
    all_sent("round_x", xrecv)
    all_sent("sums", zhsend)
    all_sent("to_run", zwrecv)
    all_sent("halves", hrecv)
    if (sent.used, due.used) != (N_SEND, N_RECV):
        raise ValueError(f"{sent.used} {due.used}")


def finish(routes, probs, rows_hbm, grads_hbm, out_tok, out_gu, out_dn, rows, grads, buf, sem):
    copies = [
        pltpu.make_async_copy(grads.at[pl.ds(0, UNITS)], out_gu.at[0], sem.at[0]),
        pltpu.make_async_copy(grads.at[pl.ds(UNITS, UNITS)], out_gu.at[1], sem.at[1]),
        pltpu.make_async_copy(grads.at[pl.ds(2 * UNITS, UNITS)], out_dn, sem.at[2]),
    ]
    loads = [
        pltpu.make_async_copy(rows_hbm, rows, sem.at[5]),
        pltpu.make_async_copy(grads_hbm, grads, sem.at[6]),
    ]
    for load in loads:
        load.start()
    n_tok = out_tok.shape[0]
    picker, _ = slots(routes, probs)
    placed = jnp.concatenate([picker, jnp.zeros((n_tok - 2 * CAP, n_tok), F32)], axis=0).T
    placed = placed[:, : 2 * CAP]
    lane = lax.broadcasted_iota(jnp.int32, (n_tok, 2 * CAP), 1)
    low = jnp.where(lane < CAP, placed, 0.0).astype(BF16)
    high = jnp.where(lane >= CAP, placed, 0.0).astype(BF16)
    loads[1].wait()
    for one in copies:
        one.start()
    loads[0].wait()
    for n, part in enumerate((low, high)):
        at = pl.ds(n * (D // 2), D // 2)
        buf[:, at] = jnp.dot(part, rows[...], preferred_element_type=F32).astype(BF16)
        one = pltpu.make_async_copy(buf.at[:, at], out_tok.at[:, at], sem.at[3 + n])
        one.start()
        copies.append(one)
    for one in copies:
        one.wait()


def on_device(tokens_in, out_grad, routes, router_probs, gate_up, down_proj):
    vmem = pl.BlockSpec(memory_space=pltpu.VMEM)
    hbm = pl.BlockSpec(memory_space=pltpu.HBM)
    n_tok = tokens_in.shape[0]
    blocks = NY * NZ
    routes, router_probs = routes.T, router_probs.T
    rows, grads = pl.pallas_call(
        kernel,
        out_shape=(
            jax.ShapeDtypeStruct((2 * CAP, D // 2), BF16),
            jax.ShapeDtypeStruct((3 * UNITS, COLS), F32),
        ),
        in_specs=[hbm] * 6,
        out_specs=(hbm, hbm),
        scratch_shapes=[
            pltpu.VMEM(routes.shape, routes.dtype),
            pltpu.VMEM(router_probs.shape, F32),
            pltpu.VMEM((2 * CAP, D // 2), BF16),
            pltpu.VMEM((3 * UNITS, COLS), F32),
            pltpu.VMEM((n_tok, D), BF16),
            pltpu.VMEM((n_tok, D), BF16),
            pltpu.VMEM((blocks, 2 * CAP, D), BF16),
            pltpu.VMEM((3 * UNITS, D), BF16),
            pltpu.VMEM((3 * UNITS, 2 * CAP * blocks), BF16),
            pltpu.VMEM((CAP * blocks, 2 * UNITS), BF16),
            pltpu.VMEM((NY, NZ, 2 * CAP, D // 2), BF16),
            pltpu.VMEM((7 * PARTS, NZ, 2 * CAP, PART), BF16),
            pltpu.VMEM((PARTS, NZ, 2 * CAP, PART), BF16),
            pltpu.VMEM((16, 3 * UNITS, COLS), BF16),
            pltpu.VMEM((8, 3 * UNITS, COLS), BF16),
            pltpu.VMEM((6, X_ROWS, COLS), BF16),
            pltpu.VMEM((X_ROWS, COLS), BF16),
            pltpu.VMEM((X_ROWS, COLS), BF16),
            pltpu.VMEM((4, Z_ROWS, COLS), BF16),
            pltpu.VMEM((6, Z_ROWS // 2, COLS), BF16),
            pltpu.SemaphoreType.DMA((7,)),
            pltpu.SemaphoreType.DMA((N_SEND,)),
            pltpu.SemaphoreType.DMA((N_RECV,)),
        ],
        compiler_params=pltpu.CompilerParams(
            collective_id=0, has_side_effects=True, vmem_limit_bytes=56 * 2**20
        ),
        cost_estimate=pl.CostEstimate(
            flops=6 * 10**9, bytes_accessed=4 * 2**20, transcendentals=2**15
        ),
        name="expert_backward",
    )(tokens_in, out_grad, routes, router_probs, gate_up, down_proj)
    return pl.pallas_call(
        finish,
        out_shape=(
            jax.ShapeDtypeStruct(tokens_in.shape, BF16),
            jax.ShapeDtypeStruct(gate_up.shape, F32),
            jax.ShapeDtypeStruct(down_proj.shape, F32),
        ),
        in_specs=[vmem, vmem, hbm, hbm],
        out_specs=(hbm, hbm, hbm),
        scratch_shapes=[
            pltpu.VMEM((2 * CAP, D // 2), BF16),
            pltpu.VMEM((3 * UNITS, COLS), F32),
            pltpu.VMEM((n_tok, D), BF16),
            pltpu.SemaphoreType.DMA((7,)),
        ],
        name="finish",
    )(routes, router_probs, rows, grads)


def solution(mesh):
    in_specs = (
        P(("dp", "expert"), None),
        P(("dp", "expert"), None),
        P(("dp", "expert"), None),
        P(("dp", "expert"), None),
        P(None, "expert", "dp"),
        P("expert", "dp"),
    )
    out_specs = (P(("dp", "expert"), None), P(None, "expert", "dp"), P("expert", "dp"))
    return jax.shard_map(
        on_device, mesh=mesh, in_specs=in_specs, out_specs=out_specs, check_vma=False
    )
```
